256 devices in a mesh: ctx: 4 (over y_hi, core), row: 8 (over x, y_lo), tp: 8 (over z).
Axes of the slice: x: 4, y: 4 (y_hi: 2, y_lo: 2; y = y_hi * 2 + y_lo), z: 8, core: 2. Of those that a mesh axis runs over, the one named last changes fastest.
Arguments:
- prefill_query: bfloat16 [8, 1024, 8192], P('row', 'ctx', 'tp')
- prefix_keys: bfloat16 [8, 8192, 1024], P('row', 'ctx', 'tp')
- prefix_values: bfloat16 [8, 8192, 1024], P('row', 'ctx', 'tp'), may hold values from -6 to 6
- span_keys: bfloat16 [8, 1024, 1024], P('row', 'ctx', 'tp'), may hold values from -6 to 6
- span_values: bfloat16 [8, 1024, 1024], P('row', 'ctx', 'tp'), may hold values from -6 to 6
- prefix_len: int32 [8], replicated, may hold values from 1 to 8192, as said below
- context_len: int32 [8], replicated, may hold values from 2 to 9216, as said below
- hidden: bfloat16 [256, 8192], P('tp', ('ctx', 'row'))
- qkv_weight: bfloat16 [8192, 8, 1280], P(('ctx', 'row'), 'tp')
- out_weight: bfloat16 [8192, 8192], P('tp', ('ctx', 'row'))
- cache_keys: bfloat16 [256, 1024, 1024], P(('ctx', 'row'), None, 'tp')
- cache_values: bfloat16 [256, 1024, 1024], P(('ctx', 'row'), None, 'tp'), may hold values from -6 to 6
- row_context: int32 [256], replicated, may hold values from 0 to 7
- cache_len: int32 [256], replicated, may hold values from 2 to 1024, as said below
Outputs:
- prefill_out: bfloat16 [8, 1024, 8192], P('row', 'ctx', 'tp')
- step_out: bfloat16 [2, 256, 8192], P(None, 'tp', ('ctx', 'row'))
The draws below stay inside these ranges and needn't reach their ends.
Inputs may be any that keep to these rules, and one draw needn't show every extreme that they name: `prefix_len`: every context has at least one live slot before its block, and one context has all 8192. context_len - prefix_len is from 1 to 1024 for every context; the context that has all 8192 prefix slots also has a full block. `cache_len`: every proof row has at least two live cache slots; one row has all 1024.
All inputs are finite; a program needn't handle non-finite values.
Results may differ from the reference program's by a relative error of at most 0.04.
Values may be sent and summed in bfloat16 or wider, within the bound.
A program may use at most 128 MiB of HBM per device.

```python
import jax
import jax.numpy as jnp
from jax import lax

D = 8192
QH = 64
KVH = 8
HD = 128
GROUP = 8
SPAN = 1024
PAST = 8192
CACHE = 1024
STEPS = 2
NCTX = 8
ROWS = 256


def shared_keys(key):
    return jnp.clip(jax.random.normal(key, (NCTX, PAST, KVH * HD), jnp.float32), -6.0, 6.0)


def length_pair(key):
    key_one, key_two, key_three = jax.random.split(key, 3)
    prefix_row_count = jax.random.randint(key_one, (NCTX,), 1, PAST + 1)
    block_count = jax.random.randint(key_two, (NCTX,), 1, SPAN + 1)
    chosen = jax.random.randint(key_three, (), 0, NCTX)
    prefix_row_count = prefix_row_count.at[chosen].set(PAST)
    block_count = block_count.at[chosen].set(SPAN)
    return (prefix_row_count, prefix_row_count + block_count)


def draw_prefix_len(key, part):
    return length_pair(key)[0]


def draw_context_len(key, part):
    return length_pair(key)[1]


def draw_prefix_keys(key, part):
    base = shared_keys(key)
    return base.astype(jnp.bfloat16)


def draw_prefill_query(key, part):
    key = jax.random.fold_in(key, 12)
    fresh = jnp.clip(jax.random.normal(key, (NCTX, SPAN, QH * HD), jnp.float32), -6.0, 6.0)
    return fresh.astype(jnp.bfloat16)


def draw_cache_len(key, part):
    key = jax.random.fold_in(key, 13)
    key_one, key_two, key_three = jax.random.split(key, 3)
    left_draw = jax.random.randint(key_one, (ROWS,), 0, CACHE - 1)
    right_draw = jax.random.randint(key_two, (ROWS,), 0, CACHE - 1)
    lengths = 2 + left_draw * right_draw // CACHE
    chosen = jax.random.randint(key_three, (), 0, ROWS)
    return lengths.at[chosen].set(CACHE)


def draw_hidden(key, part):
    key = jax.random.fold_in(key, 14)
    base = jnp.clip(jax.random.normal(key, (ROWS, D), jnp.float32), -6.0, 6.0)
    return base.astype(jnp.bfloat16)


def draw_qkv_weight(key, part):
    key = jax.random.fold_in(key, 15)
    base = jnp.clip(jax.random.normal(key, (D, KVH, (GROUP + 2) * HD), jnp.float32), -6.0, 6.0) * D ** (-0.5)
    return base.astype(jnp.bfloat16)


def draw_out_weight(key, part):
    key = jax.random.fold_in(key, 17)
    base = jnp.clip(jax.random.normal(key, (QH * HD, D), jnp.float32), -6.0, 6.0) * (4.0 * (QH * HD) ** (-0.5))
    return base.astype(jnp.bfloat16)


def draw_cache_keys(key, part):
    key = jax.random.fold_in(key, 16)
    base = jnp.clip(jax.random.normal(key, (ROWS, CACHE, KVH * HD), jnp.float32), -6.0, 6.0)
    return base.astype(jnp.bfloat16)


def place_ends(array, key, smallest, top_value):
    spot = [jax.random.randint(jax.random.fold_in(key, axis), (), 0, length) for axis, length in enumerate(array.shape)]
    main_axis = array.shape.index(max(array.shape))
    beside = spot[:main_axis] + [(spot[main_axis] + 1) % array.shape[main_axis]] + spot[main_axis + 1:]
    return array.at[tuple(spot)].set(smallest).at[tuple(beside)].set(top_value)


def levels(own_key, dims, cuts, smallest, high):
    def one(position, parts):
        heights = jax.random.uniform(jax.random.fold_in(jax.random.fold_in(own_key, 6), position), (parts,), jnp.float32, smallest / len(cuts), high / len(cuts))
        return jnp.repeat(jnp.exp(heights), dims[position] // parts).reshape((-1,) + (1,) * (len(dims) - position - 1))

    gain = one(*cuts[0])
    for cut in cuts[1:]:
        gain = gain * one(*cut)
    return gain


def normal_values(own_key, extent, deviation, limit, pieces=(), held_as=jnp.bfloat16):
    values = jax.random.normal(own_key, extent, jnp.float32) * deviation
    if len(pieces) > 0:
        values = levels(own_key, extent, pieces, -0.22, 0.18) * values
    return jnp.clip(values, min=-limit, max=limit).astype(held_as)


def setup_inputs(seed: int = 0) -> dict:
    streams_of = jax.random.split(jax.random.key(seed), 15)
    prefill_query = draw_prefill_query(jax.random.fold_in(streams_of[14], 71), 0)
    prefix_keys = draw_prefix_keys(jax.random.fold_in(streams_of[14], 71), 0)
    prefix_values = normal_values(streams_of[2], (NCTX, PAST, KVH * HD), 1.0, 6.0, ((0, 8), (1, 4), (2, 8)))
    span_keys = normal_values(streams_of[3], (NCTX, SPAN, KVH * HD), 1.0, 6.0, ((0, 8), (1, 4), (2, 8)))
    span_values = normal_values(streams_of[4], (NCTX, SPAN, KVH * HD), 1.0, 6.0, ((0, 8), (1, 4), (2, 8)))
    prefix_len = draw_prefix_len(jax.random.fold_in(streams_of[14], 71), 0)
    context_len = draw_context_len(jax.random.fold_in(streams_of[14], 71), 0)
    hidden = draw_hidden(jax.random.fold_in(streams_of[14], 71), 0)
    qkv_weight = draw_qkv_weight(jax.random.fold_in(streams_of[14], 71), 0)
    out_weight = draw_out_weight(jax.random.fold_in(streams_of[14], 71), 0)
    cache_keys = draw_cache_keys(jax.random.fold_in(streams_of[14], 71), 0)
    cache_values = normal_values(streams_of[11], (ROWS, CACHE, KVH * HD), 1.0, 6.0, ((0, 32), (2, 8)))
    row_context = place_ends(jax.random.randint(streams_of[12], (ROWS,), 0, NCTX), jax.random.fold_in(streams_of[12], 1), 0, NCTX - 1).astype(jnp.int32)
    cache_len = draw_cache_len(jax.random.fold_in(streams_of[14], 71), 0)
    return dict(prefill_query=prefill_query, prefix_keys=prefix_keys, prefix_values=prefix_values, span_keys=span_keys, span_values=span_values, prefix_len=prefix_len, context_len=context_len, hidden=hidden, qkv_weight=qkv_weight, out_weight=out_weight, cache_keys=cache_keys, cache_values=cache_values, row_context=row_context, cache_len=cache_len)


NEGATIVE = -1e30


def weigh_scores(scores, usable):
    scores = jnp.where(usable, scores, NEGATIVE)
    peak = jnp.max(scores, -1, keepdims=True)
    expon = jnp.where(usable, jnp.exp(scores - peak), 0.0)
    weight_sum = jnp.sum(expon, -1)
    rounded = lax.optimization_barrier(expon.astype(jnp.bfloat16)).astype(jnp.float32)
    return rounded, weight_sum


def prefill_context(input_rows_list):
    query_matrix, prefix_key_rows, prefix_value_rows, split_key_rows, split_value_rows, prefix_row_count, total_row_count = input_rows_list
    key_row_matrix = jnp.concatenate([prefix_key_rows, split_key_rows], 0)
    value_rows = jnp.concatenate([prefix_value_rows, split_value_rows], 0)
    positions = jnp.arange(PAST + SPAN)
    query_pos = jnp.arange(SPAN)
    block_pos = positions - PAST
    usable = jnp.where(positions[None, :] < PAST, positions[None, :] < prefix_row_count,
                       (block_pos[None, :] <= query_pos[:, None]) & (block_pos[None, :] < total_row_count - prefix_row_count))
    query_heads = query_matrix.reshape(SPAN, KVH, GROUP, HD).transpose(1, 0, 2, 3)
    key_heads = key_row_matrix.reshape(PAST + SPAN, KVH, HD).transpose(1, 0, 2)
    value_heads = value_rows.reshape(PAST + SPAN, KVH, HD).transpose(1, 0, 2)

    def per_kv_head(operands):
        qgroup, kgroup, vgroup = operands
        scores = jnp.einsum('cgd,ld->cgl', qgroup.astype(jnp.float32), kgroup.astype(jnp.float32)) * (HD ** -0.5)
        rounded, weight_sum = weigh_scores(scores, usable[:, None, :])
        summed = jnp.einsum('cgl,ld->cgd', rounded, vgroup.astype(jnp.float32))
        return summed / weight_sum[..., None]

    result = lax.map(per_kv_head, (query_heads, key_heads, value_heads))
    return result.transpose(1, 0, 2, 3).reshape(SPAN, QH * HD).astype(jnp.bfloat16)


def reference(prefill_query, prefix_keys, prefix_values, span_keys, span_values, prefix_len, context_len,
              hidden, qkv_weight, out_weight, cache_keys, cache_values, row_context, cache_len):
    prefill_out = lax.map(prefill_context, (prefill_query, prefix_keys, prefix_values, span_keys, span_values,
                                            prefix_len, context_len))
    valid_counts = (context_len - prefix_len)[row_context]
    span_usable = jnp.arange(SPAN)[None, :] < valid_counts[:, None]
    cache_usable = jnp.arange(CACHE)[None, :] < cache_len[:, None]
    weight_flat = qkv_weight.reshape(D, KVH * (GROUP + 2) * HD)
    span_k = span_keys.reshape(NCTX, SPAN, KVH, HD).transpose(2, 0, 1, 3)
    span_v = span_values.reshape(NCTX, SPAN, KVH, HD).transpose(2, 0, 1, 3)
    cache_k = cache_keys.reshape(ROWS, CACHE, KVH, HD).transpose(2, 0, 1, 3)
    cache_v = cache_values.reshape(ROWS, CACHE, KVH, HD).transpose(2, 0, 1, 3)
    state = hidden
    new_keys = []
    new_values = []
    outputs = []
    for step_index in range(STEPS):
        projected = jnp.dot(state, weight_flat, preferred_element_type=jnp.float32).astype(jnp.bfloat16)
        projected = projected.reshape(ROWS, KVH, GROUP + 2, HD)
        new_keys.append(projected[:, :, GROUP])
        new_values.append(projected[:, :, GROUP + 1])
        fresh_k = jnp.stack(new_keys, 1).transpose(2, 0, 1, 3)
        fresh_v = jnp.stack(new_values, 1).transpose(2, 0, 1, 3)
        query_heads = projected[:, :, :GROUP].transpose(1, 0, 2, 3)
        fresh_usable = jnp.ones((ROWS, step_index + 1), bool)
        usable = jnp.concatenate([span_usable, cache_usable, fresh_usable], 1)

        def per_kv_head(operands):
            qgroup, sk, sv, hk, hv, fk, fv = operands
            key_row_matrix = jnp.concatenate([sk[row_context], hk, fk], 1)
            value_rows = jnp.concatenate([sv[row_context], hv, fv], 1)
            scores = jnp.einsum('rgd,rld->rgl', qgroup.astype(jnp.float32), key_row_matrix.astype(jnp.float32)) * (HD ** -0.5)
            rounded, weight_sum = weigh_scores(scores, usable[:, None, :])
            summed = jnp.einsum('rgl,rld->rgd', rounded, value_rows.astype(jnp.float32))
            return summed / weight_sum[..., None]

        attended = lax.map(per_kv_head, (query_heads, span_k, span_v, cache_k, cache_v, fresh_k, fresh_v))
        attended = attended.transpose(1, 0, 2, 3).reshape(ROWS, QH * HD).astype(jnp.bfloat16)
        result = jnp.dot(attended, out_weight, preferred_element_type=jnp.float32).astype(jnp.bfloat16)
        outputs.append(result)
        state = (state.astype(jnp.float32) + result.astype(jnp.float32)).astype(jnp.bfloat16)
    return prefill_out, jnp.stack(outputs, 0)
```

```python
import jax
import jax.numpy as jnp
from jax import lax
from jax.experimental import pallas as pl
from jax.experimental.pallas import tpu as pltpu
from jax.sharding import PartitionSpec as P

HD = 128
GROUP = 8
STEPS = 2
SPAN = 1024
CACHE = 1024
PIECE = 2048
DRW = 8
TAIL = 2 * SPAN
KEYS = TAIL + 128
UNIT = 1024
NEGATIVE = -1e30
SCALE = HD ** (-0.5)
LOG2E = 1.4426950408889634
F32 = jnp.float32
BF16 = jnp.bfloat16
MESH = pl.DeviceIdType.MESH


def nt_dot(a, b):
    return lax.dot_general(a, b, (((1,), (1,)), ((), ())), preferred_element_type=F32)


def kernel(
    prefix_len, context_len, row_context, cache_len,
    q_hbm, pk_hbm, pv_hbm, sk_hbm, sv_hbm, hid_hbm, wq_hbm, wo_hbm, ck_hbm, cv_hbm,
    pre_out, step_out,
    q, kv, kx, vx, k0, span, kd, vd, bias, span_bias, wq, wo,
    state, xall, part, pair, rs_send, rs_recv, heads, new_kv, att_o, att_send, att_all, z_send, z_recv,
    m_ref, acc_ref,
    local_sem, z_ssem, z_rsem, pr_ssem, pr_rsem, rs_ssem, rs_rsem, at_ssem, at_rsem, fw_ssem, fw_rsem,
    rz_ssem, rz_rsem, k0_ssem, k0_rsem, sy_ssem, sy_rsem, sx_ssem, sx_rsem, sf_ssem, sf_rsem,
    pf_ssem, pf_rsem,
):
    ctx = lax.axis_index("ctx")
    row = lax.axis_index("row")
    tp = lax.axis_index("tp")
    core = ctx % 2
    y_hi = ctx // 2
    x = row // 2
    y_lo = row % 2
    y = y_hi * 2 + y_lo
    me = y_hi * 8 + row

    def plane(e):
        t = (me + e) % 16
        return t, {"ctx": (t // 8) * 2 + core, "row": t % 8}

    def along_y(e):
        t = (y + e) % 4
        return {"ctx": (t // 2) * 2 + core, "row": x * 2 + t % 2}

    def along_x(e):
        return {"row": ((x + e) % 4) * 2 + y_lo}

    def along_z(e):
        t = (tp + e) % 8
        return t, {"tp": t}

    other_core = {"ctx": y_hi * 2 + 1 - core}
    far = {"ctx": (1 - y_hi) * 2 + core}
    diagonal = {"ctx": (1 - y_hi) * 2 + 1 - core}
    other_ctx = y_hi * 2 + 1 - core
    far_ctx = (1 - y_hi) * 2 + core
    diagonal_ctx = (1 - y_hi) * 2 + 1 - core

    def remote(src, dst, ssem, rsem, device):
        return pltpu.make_async_remote_copy(
            src_ref=src, dst_ref=dst, send_sem=ssem, recv_sem=rsem, device_id=device, device_id_type=MESH
        )

    locals_ = [
        (hid_hbm.at[0], state.at[0]),
        (wq_hbm, wq),
        (pk_hbm, kv.at[ctx, 0]),
        (pv_hbm, kv.at[ctx, 1]),
        (sk_hbm, span.at[core, x, y_hi, y_lo, 0]),
        (sv_hbm, span.at[core, x, y_hi, y_lo, 1]),
        (q_hbm, q),
        (wo_hbm, wo),
        (ck_hbm, kd.at[:, pl.ds(SPAN, CACHE)]),
        (cv_hbm, vd.at[:, pl.ds(SPAN, CACHE)]),
        (pk_hbm.at[pl.ds(0, 16)], k0.at[ctx]),
    ]
    locals_ = [pltpu.make_async_copy(a, b, local_sem.at[i]) for i, (a, b) in enumerate(locals_)]
    for c in locals_:
        c.start()

    barrier = pltpu.get_barrier_semaphore()

    def greet(device):
        pl.semaphore_signal(barrier, inc=1, device_id=device, device_id_type=MESH)

    def greet_plane(e, _):
        greet(plane(e)[1])
        return 0

    def greet_z(e, _):
        greet(along_z(e)[1])
        return 0

    lax.fori_loop(1, 16, greet_plane, 0)
    lax.fori_loop(1, 8, greet_z, 0)
    greet(other_core)
    greet(diagonal)
    pl.semaphore_wait(barrier, 24)

    def hidden_copy(s, e):
        return remote(state.at[s], xall.at[s, tp], z_ssem.at[s, e], z_rsem.at[s, e], along_z(e)[1])

    def hidden_start(s):
        def body(e, _):
            hidden_copy(s, e).start()
            return 0
        lax.fori_loop(1, 8, body, 0)
        xall[s, tp] = state[s]

    def hidden_wait(s):
        def body(e, _):
            hidden_copy(s, e).wait()
            return 0
        lax.fori_loop(1, 8, body, 0)

    def pair_copy(s):
        return remote(part.at[s, 1 - core], pair.at[s], pr_ssem.at[s], pr_rsem.at[s], other_core)

    def rs_copy(s, e):
        t, device = plane(e)
        return remote(rs_send.at[s, t], rs_recv.at[s, me], rs_ssem.at[s, e], rs_rsem.at[s, e], device)

    def att_copy(s, e):
        return remote(att_send.at[s], att_all.at[s, core, me], at_ssem.at[s, e], at_rsem.at[s, e], plane(e)[1])

    def att_forward(s):
        return remote(att_all.at[s, core], att_all.at[s, core], fw_ssem.at[s], fw_rsem.at[s], other_core)

    def out_copy(s, e):
        t, device = along_z(e)
        block = ((t // 2) % 2 * 2 + t // 4) * 2 + t % 2
        return remote(z_send.at[s, block], z_recv.at[s, tp], rz_ssem.at[s, e], rz_rsem.at[s, e], device)

    k0_copies = [
        remote(k0.at[ctx], k0.at[ctx], k0_ssem.at[i], k0_rsem.at[i], device)
        for i, device in enumerate((other_core, far, diagonal))
    ]
    span_y = [
        remote(
            span.at[core, x, y_hi, y_lo], span.at[core, x, y_hi, y_lo], sy_ssem.at[e], sy_rsem.at[e], along_y(e + 1)
        )
        for e in range(3)
    ]
    span_x = [
        remote(span.at[core, x], span.at[core, x], sx_ssem.at[e], sx_rsem.at[e], along_x(e + 1)) for e in range(3)
    ]
    span_forward = remote(span.at[core], span.at[core], sf_ssem, sf_rsem, other_core)
    prefix_core = remote(kv.at[ctx], kv.at[ctx], pf_ssem.at[0], pf_rsem.at[0], other_core)
    prefix_far = remote(kv.at[ctx], kv.at[ctx], pf_ssem.at[1], pf_rsem.at[1], far)
    prefix_forward = remote(kv.at[far_ctx], kv.at[far_ctx], pf_ssem.at[2], pf_rsem.at[2], other_core)

    def project(s):
        out = jnp.dot(xall[s].reshape(256, 256), wq[...], preferred_element_type=F32).reshape(32, 8, 1280)
        both = jnp.concatenate([out[:, :, :640], out[:, :, 640:]], 1).astype(BF16)
        for j in range(4):
            part[s, j % 2, pl.ds((j // 2) * 8, 8)] = both[j * 8:j * 8 + 8]
        pair_copy(s).start()

    def scatter(s):
        pair_copy(s).wait()
        rs_send[s] = (part[s, core].astype(F32) + pair[s].astype(F32)).astype(BF16)

        def body(e, _):
            rs_copy(s, e).start()
            return 0
        lax.fori_loop(1, 16, body, 0)
        rs_recv[s, me] = rs_send[s, me]

    def gather_rows(s):
        def body(e, _):
            rs_copy(s, e).wait()
            return 0
        lax.fori_loop(1, 16, body, 0)
        total = jnp.sum(rs_recv[s].astype(F32), 0).astype(BF16).astype(F32)
        for i in range(5):
            heads[i] = total[0:8, i * HD:(i + 1) * HD]
        for i in range(3):
            heads[5 + i] = total[8:16, i * HD:(i + 1) * HD]
        new_kv[s, 0] = total[8:16, 3 * HD:4 * HD]
        new_kv[s, 1] = total[8:16, 4 * HD:5 * HD]
        spot = lax.broadcasted_iota(jnp.int32, (16, HD), 0)
        for r in range(DRW):
            for which, buffer in ((0, kd), (1, vd)):
                fresh = jnp.zeros((16, HD), F32)
                for t in range(s + 1):
                    fresh = jnp.where(spot == t, new_kv[t, which, pl.ds(r, 1), :], fresh)
                buffer[r, pl.ds(TAIL, 16)] = fresh.astype(BF16)

    def attend(s):
        query = jnp.stack([heads[:, r, :] for r in range(DRW)], 0).astype(BF16)
        scores = lax.dot_general(query, kd[...], (((2,), (2,)), ((0,), (0,))), preferred_element_type=F32)
        scores = scores * SCALE + bias[...]
        if s == 0:
            spot = lax.broadcasted_iota(jnp.int32, (DRW, GROUP, KEYS), 2)
            scores = jnp.where(spot == TAIL + 1, NEGATIVE, scores)
        peak = jnp.max(scores, -1, keepdims=True)
        expon = jnp.exp(scores - peak)
        total = jnp.sum(expon, -1, keepdims=True)
        summed = lax.dot_general(
            expon.astype(BF16), vd[...], (((2,), (1,)), ((0,), (0,))), preferred_element_type=F32
        )
        att_o[...] = summed / total
        for i in range(4):
            both = jnp.concatenate([att_o[:, i, :], att_o[:, 4 + i, :]], 0)
            att_send[s, :, i * HD:(i + 1) * HD] = both.astype(BF16)

        def body(e, _):
            att_copy(s, e).start()
            return 0
        lax.fori_loop(1, 16, body, 0)
        att_all[s, core, me] = att_send[s]

    def relay_attended(s):
        def body(e, _):
            att_copy(s, e).wait()
            return 0
        lax.fori_loop(1, 16, body, 0)
        att_forward(s).start()

    def out_project(s):
        att_forward(s).wait()
        rows = att_all[s].astype(F32).reshape(32, 16, 512)
        left = rows[:, 0:8].reshape(256, 512).astype(BF16)
        right = rows[:, 8:16].reshape(256, 512).astype(BF16)
        out = jnp.dot(left, wo[0:512], preferred_element_type=F32)
        out = out + jnp.dot(right, wo[512:1024], preferred_element_type=F32)
        z_send[s] = out.astype(BF16).reshape(8, 32, 256)

        def body(e, _):
            out_copy(s, e).start()
            return 0
        lax.fori_loop(1, 8, body, 0)
        z_recv[s, tp] = z_send[s, ((tp // 2) % 2 * 2 + tp // 4) * 2 + tp % 2]

    def finish_step(s):
        def body(e, _):
            out_copy(s, e).wait()
            return 0
        lax.fori_loop(1, 8, body, 0)
        result = jnp.sum(z_recv[s].astype(F32), 0).astype(BF16)
        step_out[s] = result
        if s + 1 < STEPS:
            state[s + 1] = (state[s].astype(F32) + result.astype(F32)).astype(BF16)

    def pick_span():
        def body(r, _):
            c = row_context[me_rows + r]
            for k in range(2):
                for h in range(2):
                    at = (h * 2 + k) * 256
                    kd[r, pl.ds(at, 256)] = span[k, c // 2, h, c % 2, 0]
                    vd[r, pl.ds(at, 256)] = span[k, c // 2, h, c % 2, 1]
            return 0
        lax.fori_loop(0, DRW, body, 0)

    me_rows = (ctx * 8 + row) * DRW

    def decode_bias():
        spot = lax.broadcasted_iota(jnp.int32, (GROUP, KEYS), 1)

        def body(r, _):
            c = row_context[me_rows + r]
            valid = context_len[c] - prefix_len[c]
            live = cache_len[me_rows + r]
            end = jnp.where(spot < SPAN, valid, jnp.where(spot < TAIL, SPAN + live, TAIL + STEPS))
            bias[r] = jnp.where(spot < end, 0.0, NEGATIVE)
            kd[r, pl.ds(TAIL, 128)] = jnp.zeros((128, HD), BF16)
            vd[r, pl.ds(TAIL, 128)] = jnp.zeros((128, HD), BF16)
            return 0
        lax.fori_loop(0, DRW, body, 0)

    def prefill_start():
        m_ref[...] = jnp.full(m_ref.shape, NEGATIVE, F32)
        acc_ref[...] = jnp.zeros(acc_ref.shape, F32)
        at = lax.broadcasted_iota(jnp.int32, (256, SPAN), 0) + ctx * 256
        spot = lax.broadcasted_iota(jnp.int32, (256, SPAN), 1)
        valid = context_len[row] - prefix_len[row]
        span_bias[...] = jnp.where((spot <= at) & (spot < valid), 0.0, NEGATIVE)

    def prepare(piece):
        spot = lax.broadcasted_iota(jnp.int32, (PIECE, HD), 0) + piece * PIECE
        live = spot < prefix_len[row]
        first = k0[0, 0:1, :].astype(F32)
        kx[...] = jnp.where(live, kv[piece, 0].astype(F32), first).astype(BF16)
        vx[:, 0:HD] = jnp.where(live, kv[piece, 1].astype(F32), 0.0).astype(BF16)
        vx[:, HD:2 * HD] = jnp.where(live, 1.0, 0.0).astype(BF16)

    def update(h, keys, values, mask):
        query = q[:, pl.ds(pl.multiple_of(h * HD, HD), HD)]
        scores = nt_dot(query, keys)
        if mask is not None:
            scores = scores + mask
        old = m_ref[h]
        new = jnp.maximum(old, jnp.max(scores, 1, keepdims=True))
        expon = jnp.exp2((scores - new[:, 0:1]) * (SCALE * LOG2E)).astype(BF16)
        rescale = jnp.exp2((old - new) * (SCALE * LOG2E))
        m_ref[h] = new
        acc_ref[h] = acc_ref[h] * jnp.concatenate([rescale, rescale], 1) + jnp.dot(
            expon, values, preferred_element_type=F32
        )

    def unit(j):
        def body(h, _):
            update(h, kx[pl.ds(j * UNIT, UNIT)], vx[pl.ds(j * UNIT, UNIT)], None)
            return 0
        lax.fori_loop(0, GROUP, body, 0)

    def span_unit():
        for i in range(4):
            kx[pl.ds(i * 256, 256)] = span[i % 2, x, i // 2, y_lo, 0]
            vx[pl.ds(i * 256, 256), 0:HD] = span[i % 2, x, i // 2, y_lo, 1]
        vx[:, HD:2 * HD] = jnp.ones((PIECE, HD), BF16)

        def body(h, _):
            update(h, kx[pl.ds(0, SPAN)], vx[pl.ds(0, SPAN)], span_bias[...])
            return 0
        lax.fori_loop(0, GROUP, body, 0)

    def prefill_end():
        for h in range(GROUP):
            acc = acc_ref[h]
            pre_out[:, h * HD:(h + 1) * HD] = (acc[:, 0:HD] / acc[:, HD:2 * HD]).astype(BF16)

    locals_[0].wait()
    hidden_start(0)
    locals_[10].wait()
    for c in k0_copies:
        c.start()
    locals_[4].wait()
    locals_[5].wait()
    for c in span_y:
        c.start()
    locals_[2].wait()
    locals_[3].wait()
    prefix_core.start()
    prefix_far.start()
    locals_[1].wait()
    hidden_wait(0)
    project(0)
    for c in k0_copies:
        c.wait()
    prefill_start()
    prepare(ctx)
    scatter(0)
    for c in span_y:
        c.wait()
    for c in span_x:
        c.start()
    locals_[6].wait()
    unit(0)
    unit(1)
    decode_bias()
    gather_rows(0)
    prefix_core.wait()
    prepare(other_ctx)
    unit(0)
    for c in span_x:
        c.wait()
    span_forward.start()
    prefix_far.wait()
    prefix_forward.start()
    unit(1)
    span_forward.wait()
    pick_span()
    locals_[8].wait()
    locals_[9].wait()
    attend(0)
    locals_[7].wait()
    prepare(far_ctx)
    unit(0)
    relay_attended(0)
    out_project(0)
    unit(1)
    finish_step(0)
    hidden_start(1)
    prefix_forward.wait()
    prepare(diagonal_ctx)
    hidden_wait(1)
    project(1)
    scatter(1)
    unit(0)
    gather_rows(1)
    attend(1)
    unit(1)
    relay_attended(1)
    out_project(1)
    span_unit()
    prefill_end()
    finish_step(1)


def local(
    prefill_query, prefix_keys, prefix_values, span_keys, span_values, prefix_len, context_len,
    hidden, qkv_weight, out_weight, cache_keys, cache_values, row_context, cache_len,
):
    dma = pltpu.SemaphoreType.DMA
    smem = pl.BlockSpec(memory_space=pltpu.SMEM)
    anywhere = pl.BlockSpec(memory_space=pl.ANY)
    vmem = pl.BlockSpec(memory_space=pltpu.VMEM)
    pre, steps = pl.pallas_call(
        kernel,
        out_shape=(
            jax.ShapeDtypeStruct((256, GROUP * HD), BF16),
            jax.ShapeDtypeStruct((STEPS, 32, 256), BF16),
        ),
        in_specs=[smem] * 4 + [anywhere] * 10,
        out_specs=(vmem, vmem),
        scratch_shapes=[
            pltpu.VMEM((256, GROUP * HD), BF16),
            pltpu.VMEM((4, 2, PIECE, HD), BF16),
            pltpu.VMEM((PIECE, HD), BF16),
            pltpu.VMEM((PIECE, 2 * HD), BF16),
            pltpu.VMEM((4, 16, HD), BF16),
            pltpu.VMEM((2, 4, 2, 2, 2, 256, HD), BF16),
            pltpu.VMEM((DRW, KEYS, HD), BF16),
            pltpu.VMEM((DRW, KEYS, HD), BF16),
            pltpu.VMEM((DRW, GROUP, KEYS), F32),
            pltpu.VMEM((256, SPAN), F32),
            pltpu.VMEM((256, 1280), BF16),
            pltpu.VMEM((1024, 256), BF16),
            pltpu.VMEM((STEPS, 32, 256), BF16),
            pltpu.VMEM((STEPS, 8, 32, 256), BF16),
            pltpu.VMEM((STEPS, 2, 16, 16, 640), BF16),
            pltpu.VMEM((STEPS, 16, 16, 640), BF16),
            pltpu.VMEM((STEPS, 16, 16, 640), BF16),
            pltpu.VMEM((STEPS, 16, 16, 640), BF16),
            pltpu.VMEM((GROUP, DRW, HD), F32),
            pltpu.VMEM((STEPS, 2, DRW, HD), F32),
            pltpu.VMEM((DRW, GROUP, HD), F32),
            pltpu.VMEM((STEPS, 16, 512), BF16),
            pltpu.VMEM((STEPS, 2, 16, 16, 512), BF16),
            pltpu.VMEM((STEPS, 8, 32, 256), BF16),
            pltpu.VMEM((STEPS, 8, 32, 256), BF16),
            pltpu.VMEM((GROUP, 256, HD), F32),
            pltpu.VMEM((GROUP, 256, 2 * HD), F32),
            dma((11,)),
            dma((STEPS, 8)), dma((STEPS, 8)),
            dma((STEPS,)), dma((STEPS,)),
            dma((STEPS, 16)), dma((STEPS, 16)),
            dma((STEPS, 16)), dma((STEPS, 16)),
            dma((STEPS,)), dma((STEPS,)),
            dma((STEPS, 8)), dma((STEPS, 8)),
            dma((3,)), dma((3,)),
            dma((3,)), dma((3,)),
            dma((3,)), dma((3,)),
            dma, dma,
            dma((3,)), dma((3,)),
        ],
        compiler_params=pltpu.CompilerParams(
            collective_id=0, has_side_effects=True, vmem_limit_bytes=56 * 1024 * 1024
        ),
        name="layer",
    )(
        prefix_len, context_len, row_context, cache_len,
        prefill_query[0], prefix_keys[0], prefix_values[0], span_keys[0], span_values[0],
        hidden[None], qkv_weight.reshape(256, 1280), out_weight, cache_keys, cache_values,
    )
    return pre[None], steps


def solution(mesh):
    in_specs = (
        P("row", "ctx", "tp"),
        P("row", "ctx", "tp"),
        P("row", "ctx", "tp"),
        P("row", "ctx", "tp"),
        P("row", "ctx", "tp"),
        P(),
        P(),
        P("tp", ("ctx", "row")),
        P(("ctx", "row"), "tp", None),
        P("tp", ("ctx", "row")),
        P(("ctx", "row"), None, "tp"),
        P(("ctx", "row"), None, "tp"),
        P(),
        P(),
    )
    out_specs = (P("row", "ctx", "tp"), P(None, "tp", ("ctx", "row")))
    return jax.shard_map(local, mesh=mesh, in_specs=in_specs, out_specs=out_specs, check_vma=False)
```

```python
import jax
import jax.numpy as jnp
from jax import lax
from jax.experimental import pallas as pl
from jax.experimental.pallas import tpu as pltpu
from jax.sharding import PartitionSpec as P

HD = 128
GROUP = 8
STEPS = 2
SPAN = 1024
CACHE = 1024
PIECE = 2048
DRW = 8
TAIL = 2 * SPAN
KEYS = TAIL + 128
UNIT = 1024
CHUNK = 256
NEGATIVE = -1e30
SCALE = HD ** (-0.5)
LOG2E = 1.4426950408889634
F32 = jnp.float32
BF16 = jnp.bfloat16
MESH = pl.DeviceIdType.MESH


def nt_dot(a, b):
    return lax.dot_general(a, b, (((1,), (1,)), ((), ())), preferred_element_type=F32)


def kernel(
    prefix_len, context_len, row_context, cache_len,
    q_hbm, pk_hbm, pv_hbm, sk_hbm, sv_hbm, hid_hbm, wq_hbm, wo_hbm, ck_hbm, cv_hbm,
    pre_out, step_out,
    q, kv, kx, vx, k0, span, kd, vd, bias, span_bias, wq, wo,
    state, xall, part, pair, rs_send, rs_recv, heads, new_kv, att_o, att_send, att_all, z_send, z_recv, late,
    m_ref, acc_ref,
    local_sem, z_ssem, z_rsem, pr_ssem, pr_rsem, rs_ssem, rs_rsem, at_ssem, at_rsem, fw_ssem, fw_rsem,
    rz_ssem, rz_rsem, k0_ssem, k0_rsem, s1_ssem, s1_rsem, s2_ssem, s2_rsem, sf_ssem, sf_rsem,
    pc_ssem, pc_rsem, pf_ssem, pf_rsem, pd_ssem, pd_rsem,
):
    ctx = lax.axis_index("ctx")
    row = lax.axis_index("row")
    tp = lax.axis_index("tp")
    core = ctx % 2
    y_hi = ctx // 2
    x = row // 2
    y_lo = row % 2
    y = y_hi * 2 + y_lo
    me = y_hi * 8 + row

    def plane(e):
        t = (me + e) % 16
        return t, {"ctx": (t // 8) * 2 + core, "row": t % 8}

    def along_y(e):
        t = (y + e) % 4
        return {"ctx": (t // 2) * 2 + core, "row": x * 2 + t % 2}

    def along_x(e):
        return {"row": ((x + e) % 4) * 2 + y_lo}

    def along_z(e):
        t = (tp + e) % 8
        return t, {"tp": t}

    other_core = {"ctx": y_hi * 2 + 1 - core}
    far = {"ctx": (1 - y_hi) * 2 + core}
    diagonal = {"ctx": (1 - y_hi) * 2 + 1 - core}
    other_ctx = y_hi * 2 + 1 - core
    far_ctx = (1 - y_hi) * 2 + core
    diagonal_ctx = (1 - y_hi) * 2 + 1 - core

    def remote(src, dst, ssem, rsem, device):
        return pltpu.make_async_remote_copy(
            src_ref=src, dst_ref=dst, send_sem=ssem, recv_sem=rsem, device_id=device, device_id_type=MESH
        )

    locals_ = [
        (hid_hbm.at[0], state.at[0]),
        (wq_hbm, wq),
        (pk_hbm, kv.at[ctx, 0]),
        (pv_hbm, kv.at[ctx, 1]),
        (sk_hbm, span.at[core, x, y, 0]),
        (sv_hbm, span.at[core, x, y, 1]),
        (q_hbm, q),
        (wo_hbm, wo),
        (ck_hbm, kd.at[:, pl.ds(SPAN, CACHE)]),
        (cv_hbm, vd.at[:, pl.ds(SPAN, CACHE)]),
        (pk_hbm.at[pl.ds(0, 16)], k0.at[ctx]),
    ]
    locals_ = [pltpu.make_async_copy(a, b, local_sem.at[i]) for i, (a, b) in enumerate(locals_)]
    for c in locals_:
        c.start()

    barrier = pltpu.get_barrier_semaphore()

    def greet(device):
        pl.semaphore_signal(barrier, inc=1, device_id=device, device_id_type=MESH)

    def greet_plane(e, _):
        greet(plane(e)[1])
        return 0

    def greet_z(e, _):
        greet(along_z(e)[1])
        return 0

    lax.fori_loop(1, 16, greet_plane, 0)
    lax.fori_loop(1, 8, greet_z, 0)
    greet(other_core)
    greet(diagonal)

    def hidden_copy(s, e):
        return remote(state.at[s], xall.at[s, tp], z_ssem.at[s, e], z_rsem.at[s, e], along_z(e)[1])

    def hidden_start(s):
        def body(e, _):
            hidden_copy(s, e).start()
            return 0
        lax.fori_loop(1, 8, body, 0)
        xall[s, tp] = state[s]

    def hidden_wait(s):
        def body(e, _):
            hidden_copy(s, e).wait()
            return 0
        lax.fori_loop(1, 8, body, 0)

    def pair_copy(s):
        return remote(part.at[s, 1 - core], pair.at[s], pr_ssem.at[s], pr_rsem.at[s], other_core)

    def rs_copy(s, e):
        t, device = plane(e)
        return remote(rs_send.at[s, t], rs_recv.at[s, me], rs_ssem.at[s, e], rs_rsem.at[s, e], device)

    def att_copy(s, e):
        return remote(att_send.at[s], att_all.at[s, core, me], at_ssem.at[s, e], at_rsem.at[s, e], plane(e)[1])

    def att_forward(s):
        return remote(att_all.at[s, core], att_all.at[s, core], fw_ssem.at[s], fw_rsem.at[s], other_core)

    def out_copy(s, e):
        t, device = along_z(e)
        block = ((t // 2) % 2 * 2 + t // 4) * 2 + t % 2
        return remote(z_send.at[s, block], z_recv.at[s, tp], rz_ssem.at[s, e], rz_rsem.at[s, e], device)

    k0_copies = [
        remote(k0.at[ctx], k0.at[ctx], k0_ssem.at[i], k0_rsem.at[i], device)
        for i, device in enumerate((other_core, far, diagonal))
    ]
    def span_first(e):
        piece = span.at[core, x, y]
        return (
            remote(piece, piece, s1_ssem.at[0, e], s1_rsem.at[0, e], along_x(e)),
            remote(piece, piece, s1_ssem.at[1, e], s1_rsem.at[1, e], along_y(e)),
        )

    def span_second(d, e):
        keys = span.at[core, (x + d) % 4, y, 0]
        values = span.at[core, x, (y + d) % 4, 1]
        return (
            remote(keys, keys, s2_ssem.at[0, d, e], s2_rsem.at[0, d, e], along_y(e)),
            remote(values, values, s2_ssem.at[1, d, e], s2_rsem.at[1, d, e], along_x(e)),
        )

    def span_core(d, e):
        piece = span.at[core, (x + d) % 4, (y + e) % 4]
        return remote(piece, piece, sf_ssem.at[d, e], sf_rsem.at[d, e], other_core)

    def span_open():
        for e in (1, 3, 2):
            for c in span_first(e):
                c.start()
        span_core(0, 0).start()

    def span_relay():
        for d in (1, 3, 2):
            along, across = span_first(d)
            along.wait()
            across.wait()
            for e in (1, 3, 2):
                for c in span_second(4 - d, e):
                    c.start()
            span_core(4 - d, 0).start()
            span_core(0, 4 - d).start()

    def span_own_ready():
        span_core(0, 0).wait()
        span_core(0, 2).wait()

    def span_close():
        for d in (1, 3, 2):
            for e in (1, 3, 2):
                for c in span_second(d, e):
                    c.wait()
        for d in (1, 2, 3):
            for e in (1, 2, 3):
                span_core(d, e).start()

    def span_done():
        for d in range(4):
            for e in range(4):
                if (d, e) not in ((0, 0), (0, 2)):
                    span_core(d, e).wait()

    prefix_core = remote(kv.at[ctx], kv.at[ctx], pc_ssem, pc_rsem, other_core)

    def prefix_far(i):
        chunk = kv.at[ctx, :, pl.ds(i * CHUNK, CHUNK)]
        return remote(chunk, chunk, pf_ssem.at[i], pf_rsem.at[i], far)

    def prefix_far_start(first, last):
        for i in range(first, last):
            prefix_far(i).start()

    def prefix_forward(j):
        half = kv.at[far_ctx, :, pl.ds(j * UNIT, UNIT)]
        return remote(half, half, pd_ssem.at[j], pd_rsem.at[j], other_core)

    def prefix_relay(j):
        per = UNIT // CHUNK
        for i in range(j * per, (j + 1) * per):
            prefix_far(i).wait()
        prefix_forward(j).start()

    def project(s):
        out = jnp.dot(xall[s].reshape(256, 256), wq[...], preferred_element_type=F32).reshape(32, 8, 1280)
        both = jnp.concatenate([out[:, :, :640], out[:, :, 640:]], 1).astype(BF16)
        for j in range(4):
            part[s, j % 2, pl.ds((j // 2) * 8, 8)] = both[j * 8:j * 8 + 8]
        pair_copy(s).start()

    def scatter(s):
        pair_copy(s).wait()
        rs_send[s] = (part[s, core].astype(F32) + pair[s].astype(F32)).astype(BF16)

        def body(e, _):
            rs_copy(s, e).start()
            return 0
        lax.fori_loop(1, 16, body, 0)
        rs_recv[s, me] = rs_send[s, me]

    def gather_rows(s):
        def body(e, _):
            rs_copy(s, e).wait()
            return 0
        lax.fori_loop(1, 16, body, 0)
        total = jnp.sum(rs_recv[s].astype(F32), 0).astype(BF16).astype(F32)
        for i in range(5):
            heads[i] = total[0:8, i * HD:(i + 1) * HD]
        for i in range(3):
            heads[5 + i] = total[8:16, i * HD:(i + 1) * HD]
        new_kv[s, 0] = total[8:16, 3 * HD:4 * HD]
        new_kv[s, 1] = total[8:16, 4 * HD:5 * HD]
        spot = lax.broadcasted_iota(jnp.int32, (16, HD), 0)
        for r in range(DRW):
            for which, buffer in ((0, kd), (1, vd)):
                fresh = jnp.zeros((16, HD), F32)
                for t in range(s + 1):
                    fresh = jnp.where(spot == t, new_kv[t, which, pl.ds(r, 1), :], fresh)
                buffer[r, pl.ds(TAIL, 16)] = fresh.astype(BF16)

    def query_rows():
        return jnp.stack([heads[:, r, :] for r in range(DRW)], 0).astype(BF16)

    def attend_cache():
        late[...] = lax.dot_general(
            query_rows(), kd[:, SPAN:KEYS], (((2,), (2,)), ((0,), (0,))), preferred_element_type=F32
        )

    def attend(s):
        early = lax.dot_general(
            query_rows(), kd[:, 0:SPAN], (((2,), (2,)), ((0,), (0,))), preferred_element_type=F32
        )
        scores = jnp.concatenate([early, late[...]], 2) * SCALE + bias[...]
        if s == 0:
            spot = lax.broadcasted_iota(jnp.int32, (DRW, GROUP, KEYS), 2)
            scores = jnp.where(spot == TAIL + 1, NEGATIVE, scores)
        peak = jnp.max(scores, -1, keepdims=True)
        expon = jnp.exp(scores - peak)
        total = jnp.sum(expon, -1, keepdims=True)
        summed = lax.dot_general(
            expon.astype(BF16), vd[...], (((2,), (1,)), ((0,), (0,))), preferred_element_type=F32
        )
        att_o[...] = summed / total
        for i in range(4):
            both = jnp.concatenate([att_o[:, i, :], att_o[:, 4 + i, :]], 0)
            att_send[s, :, i * HD:(i + 1) * HD] = both.astype(BF16)

        def body(e, _):
            att_copy(s, e).start()
            return 0
        lax.fori_loop(1, 16, body, 0)
        att_all[s, core, me] = att_send[s]

    def relay_attended(s):
        def body(e, _):
            att_copy(s, e).wait()
            return 0
        lax.fori_loop(1, 16, body, 0)
        att_forward(s).start()

    def out_project(s):
        att_forward(s).wait()
        rows = att_all[s].astype(F32).reshape(32, 16, 512)
        left = rows[:, 0:8].reshape(256, 512).astype(BF16)
        right = rows[:, 8:16].reshape(256, 512).astype(BF16)
        out = jnp.dot(left, wo[0:512], preferred_element_type=F32)
        out = out + jnp.dot(right, wo[512:1024], preferred_element_type=F32)
        z_send[s] = out.astype(BF16).reshape(8, 32, 256)

        def body(e, _):
            out_copy(s, e).start()
            return 0
        lax.fori_loop(1, 8, body, 0)
        z_recv[s, tp] = z_send[s, ((tp // 2) % 2 * 2 + tp // 4) * 2 + tp % 2]

    def finish_step(s):
        def body(e, _):
            out_copy(s, e).wait()
            return 0
        lax.fori_loop(1, 8, body, 0)
        result = jnp.sum(z_recv[s].astype(F32), 0).astype(BF16)
        step_out[s] = result
        if s + 1 < STEPS:
            state[s + 1] = (state[s].astype(F32) + result.astype(F32)).astype(BF16)

    def pick_span():
        def body(r, _):
            c = row_context[me_rows + r]
            for k in range(2):
                for h in range(2):
                    at = (h * 2 + k) * 256
                    kd[r, pl.ds(at, 256)] = span[k, c // 2, h * 2 + c % 2, 0]
                    vd[r, pl.ds(at, 256)] = span[k, c // 2, h * 2 + c % 2, 1]
            return 0
        lax.fori_loop(0, DRW, body, 0)

    me_rows = (ctx * 8 + row) * DRW

    def decode_bias():
        spot = lax.broadcasted_iota(jnp.int32, (GROUP, KEYS), 1)

        def body(r, _):
            c = row_context[me_rows + r]
            valid = context_len[c] - prefix_len[c]
            live = cache_len[me_rows + r]
            end = jnp.where(spot < SPAN, valid, jnp.where(spot < TAIL, SPAN + live, TAIL + STEPS))
            bias[r] = jnp.where(spot < end, 0.0, NEGATIVE)
            kd[r, pl.ds(TAIL, 128)] = jnp.zeros((128, HD), BF16)
            vd[r, pl.ds(TAIL, 128)] = jnp.zeros((128, HD), BF16)
            return 0
        lax.fori_loop(0, DRW, body, 0)

    def prefill_start():
        m_ref[...] = jnp.full(m_ref.shape, NEGATIVE, F32)
        acc_ref[...] = jnp.zeros(acc_ref.shape, F32)
        at = lax.broadcasted_iota(jnp.int32, (256, SPAN), 0) + ctx * 256
        spot = lax.broadcasted_iota(jnp.int32, (256, SPAN), 1)
        valid = context_len[row] - prefix_len[row]
        span_bias[...] = jnp.where((spot <= at) & (spot < valid), 0.0, NEGATIVE)

    def prepare(piece, j, first):
        spot = lax.broadcasted_iota(jnp.int32, (UNIT, HD), 0) + (piece * PIECE + j * UNIT)
        live = spot < prefix_len[row]
        rows = pl.ds(j * UNIT, UNIT)
        kx[...] = jnp.where(live, kv[piece, 0, rows].astype(F32), first.astype(F32)).astype(BF16)
        vx[:, 0:HD] = jnp.where(live, kv[piece, 1, rows].astype(F32), 0.0).astype(BF16)
        vx[:, HD:2 * HD] = jnp.where(live, 1.0, 0.0).astype(BF16)

    def update(h, keys, values, mask):
        scores = nt_dot(q[:, h * HD:(h + 1) * HD], keys)
        if mask is not None:
            scores = scores + mask
        old = m_ref[h]
        new = jnp.maximum(old, jnp.max(scores, 1, keepdims=True))
        expon = jnp.exp2((scores - new[:, 0:1]) * (SCALE * LOG2E)).astype(BF16)
        rescale = jnp.exp2((old - new) * (SCALE * LOG2E))
        m_ref[h] = new
        acc_ref[h] = acc_ref[h] * jnp.concatenate([rescale, rescale], 1) + jnp.dot(
            expon, values, preferred_element_type=F32
        )

    def forget_dead():
        m_ref[...] = jnp.where(ctx * PIECE < prefix_len[row], m_ref[...], NEGATIVE)

    def first_unit(j):
        prepare(ctx, j, kv[ctx, 0, 0:1, :])
        for h in range(GROUP):
            update(h, kx[...], vx[...], None)

    def unit(piece, j):
        prepare(piece, j, k0[0, 0:1, :])
        for h in range(GROUP):
            update(h, kx[...], vx[...], None)

    def span_unit():
        for i in range(4):
            kx[pl.ds(i * 256, 256)] = span[i % 2, x, i // 2 * 2 + y_lo, 0]
            vx[pl.ds(i * 256, 256), 0:HD] = span[i % 2, x, i // 2 * 2 + y_lo, 1]
        vx[:, HD:2 * HD] = jnp.ones((SPAN, HD), BF16)

        for h in range(GROUP):
            update(h, kx[...], vx[...], span_bias[...])

    def prefill_end():
        for h in range(GROUP):
            acc = acc_ref[h]
            pre_out[:, h * HD:(h + 1) * HD] = (acc[:, 0:HD] / acc[:, HD:2 * HD]).astype(BF16)

    for i in (2, 3, 6):
        locals_[i].wait()
    prefill_start()
    first_unit(0)
    for i in (0, 4, 5, 10):
        locals_[i].wait()
    pl.semaphore_wait(barrier, 24)
    hidden_start(0)
    for c in k0_copies:
        c.start()
    span_open()
    prefix_core.start()
    first_unit(1)
    forget_dead()
    locals_[1].wait()
    hidden_wait(0)
    project(0)
    for c in k0_copies:
        c.wait()
    prefix_core.wait()
    scatter(0)
    span_relay()
    unit(other_ctx, 0)
    decode_bias()
    unit(other_ctx, 1)
    span_own_ready()
    span_unit()
    gather_rows(0)
    locals_[8].wait()
    locals_[9].wait()
    span_close()
    prefix_far_start(0, 2)
    attend_cache()
    span_done()
    pick_span()
    attend(0)
    locals_[7].wait()
    relay_attended(0)
    prefix_far_start(2, 8)
    out_project(0)
    finish_step(0)
    hidden_start(1)
    prefix_relay(0)
    unit(far_ctx, 0)
    hidden_wait(1)
    project(1)
    prefix_forward(0).wait()
    scatter(1)
    unit(diagonal_ctx, 0)
    prefix_relay(1)
    unit(far_ctx, 1)
    gather_rows(1)
    attend_cache()
    attend(1)
    prefix_forward(1).wait()
    unit(diagonal_ctx, 1)
    relay_attended(1)
    out_project(1)
    prefill_end()
    finish_step(1)


def local(
    prefill_query, prefix_keys, prefix_values, span_keys, span_values, prefix_len, context_len,
    hidden, qkv_weight, out_weight, cache_keys, cache_values, row_context, cache_len,
):
    dma = pltpu.SemaphoreType.DMA
    smem = pl.BlockSpec(memory_space=pltpu.SMEM)
    anywhere = pl.BlockSpec(memory_space=pl.ANY)
    vmem = pl.BlockSpec(memory_space=pltpu.VMEM)
    pre, steps = pl.pallas_call(
        kernel,
        out_shape=(
            jax.ShapeDtypeStruct((256, GROUP * HD), BF16),
            jax.ShapeDtypeStruct((STEPS, 32, 256), BF16),
        ),
        in_specs=[smem] * 4 + [anywhere] * 10,
        out_specs=(vmem, vmem),
        scratch_shapes=[
            pltpu.VMEM((256, GROUP * HD), BF16),
            pltpu.VMEM((4, 2, PIECE, HD), BF16),
            pltpu.VMEM((UNIT, HD), BF16),
            pltpu.VMEM((UNIT, 2 * HD), BF16),
            pltpu.VMEM((4, 16, HD), BF16),
            pltpu.VMEM((2, 4, 4, 2, 256, HD), BF16),
            pltpu.VMEM((DRW, KEYS, HD), BF16),
            pltpu.VMEM((DRW, KEYS, HD), BF16),
            pltpu.VMEM((DRW, GROUP, KEYS), F32),
            pltpu.VMEM((256, SPAN), F32),
            pltpu.VMEM((256, 1280), BF16),
            pltpu.VMEM((1024, 256), BF16),
            pltpu.VMEM((STEPS, 32, 256), BF16),
            pltpu.VMEM((STEPS, 8, 32, 256), BF16),
            pltpu.VMEM((STEPS, 2, 16, 16, 640), BF16),
            pltpu.VMEM((STEPS, 16, 16, 640), BF16),
            pltpu.VMEM((STEPS, 16, 16, 640), BF16),
            pltpu.VMEM((STEPS, 16, 16, 640), BF16),
            pltpu.VMEM((GROUP, DRW, HD), F32),
            pltpu.VMEM((STEPS, 2, DRW, HD), F32),
            pltpu.VMEM((DRW, GROUP, HD), F32),
            pltpu.VMEM((STEPS, 16, 512), BF16),
            pltpu.VMEM((STEPS, 2, 16, 16, 512), BF16),
            pltpu.VMEM((STEPS, 8, 32, 256), BF16),
            pltpu.VMEM((STEPS, 8, 32, 256), BF16),
            pltpu.VMEM((DRW, GROUP, KEYS - SPAN), F32),
            pltpu.VMEM((GROUP, 256, HD), F32),
            pltpu.VMEM((GROUP, 256, 2 * HD), F32),
            dma((11,)),
            dma((STEPS, 8)), dma((STEPS, 8)),
            dma((STEPS,)), dma((STEPS,)),
            dma((STEPS, 16)), dma((STEPS, 16)),
            dma((STEPS, 16)), dma((STEPS, 16)),
            dma((STEPS,)), dma((STEPS,)),
            dma((STEPS, 8)), dma((STEPS, 8)),
            dma((3,)), dma((3,)),
            dma((2, 4)), dma((2, 4)),
            dma((2, 4, 4)), dma((2, 4, 4)),
            dma((4, 4)), dma((4, 4)),
            dma, dma,
            dma((PIECE // CHUNK,)), dma((PIECE // CHUNK,)),
            dma((2,)), dma((2,)),
        ],
        compiler_params=pltpu.CompilerParams(
            collective_id=0, has_side_effects=True, vmem_limit_bytes=56 * 1024 * 1024
        ),
        name="layer",
    )(
        prefix_len, context_len, row_context, cache_len,
        prefill_query[0], prefix_keys[0], prefix_values[0], span_keys[0], span_values[0],
        hidden[None], qkv_weight.reshape(256, 1280), out_weight, cache_keys, cache_values,
    )
    return pre[None], steps


def solution(mesh):
    in_specs = (
        P("row", "ctx", "tp"),
        P("row", "ctx", "tp"),
        P("row", "ctx", "tp"),
        P("row", "ctx", "tp"),
        P("row", "ctx", "tp"),
        P(),
        P(),
        P("tp", ("ctx", "row")),
        P(("ctx", "row"), "tp", None),
        P("tp", ("ctx", "row")),
        P(("ctx", "row"), None, "tp"),
        P(("ctx", "row"), None, "tp"),
        P(),
        P(),
    )
    out_specs = (P("row", "ctx", "tp"), P(None, "tp", ("ctx", "row")))
    return jax.shard_map(local, mesh=mesh, in_specs=in_specs, out_specs=out_specs, check_vma=False)
```

```python
import jax
import jax.numpy as jnp
from jax import lax
from jax.experimental import pallas as pl
from jax.experimental.pallas import tpu as pltpu
from jax.sharding import PartitionSpec as P

HD = 128
GROUP = 8
STEPS = 2
SPAN = 1024
CACHE = 1024
PIECE = 2048
DRW = 8
TAIL = 2 * SPAN
KEYS = TAIL + 128
UNIT = 1024
CHUNK = 256
NEGATIVE = -1e30
SCALE = HD ** (-0.5)
LOG2E = 1.4426950408889634
F32 = jnp.float32
BF16 = jnp.bfloat16
MESH = pl.DeviceIdType.MESH
Z_ORDER = (4, 3, 5, 2, 6, 1, 7)
PLANE_ORDER = (
    (2, 2), (2, 1), (2, 3), (1, 2), (3, 2), (2, 0), (0, 2), (1, 1), (1, 3), (3, 1), (3, 3), (1, 0), (3, 0), (0, 1), (0, 3)
)


def nt_dot(a, b):
    return lax.dot_general(a, b, (((1,), (1,)), ((), ())), preferred_element_type=F32)


def kernel(
    prefix_len, context_len, row_context, cache_len,
    q_hbm, pk_hbm, pv_hbm, sk_hbm, sv_hbm, hid_hbm, wq_hbm, wo_hbm, ck_hbm, cv_hbm,
    pre_out, step_out,
    q, kv, kx, vx, k0, span, kd, vd, bias, span_bias, wq, wo,
    state, xall, part, pair, rs_send, rs_recv, heads, new_kv, att_o, att_send, att_all, z_send, z_recv, late,
    m_ref, acc_ref,
    local_sem, z_ssem, z_rsem, pr_ssem, pr_rsem, rs_ssem, rs_rsem, at_ssem, at_rsem, fw_ssem, fw_rsem,
    rz_ssem, rz_rsem, k0_ssem, k0_rsem, s1_ssem, s1_rsem, s2_ssem, s2_rsem, sf_ssem, sf_rsem,
    pc_ssem, pc_rsem, pf_ssem, pf_rsem, pd_ssem, pd_rsem,
):
    ctx = lax.axis_index("ctx")
    row = lax.axis_index("row")
    tp = lax.axis_index("tp")
    core = ctx % 2
    y_hi = ctx // 2
    x = row // 2
    y_lo = row % 2
    y = y_hi * 2 + y_lo
    me = y_hi * 8 + row

    def plane(e):
        to_x, to_y = (x + e[0]) % 4, (y + e[1]) % 4
        return (to_y // 2) * 8 + to_x * 2 + to_y % 2, {"ctx": (to_y // 2) * 2 + core, "row": to_x * 2 + to_y % 2}

    def along_y(e):
        t = (y + e) % 4
        return {"ctx": (t // 2) * 2 + core, "row": x * 2 + t % 2}

    def along_x(e):
        return {"row": ((x + e) % 4) * 2 + y_lo}

    def along_z(e):
        t = (tp + e) % 8
        return t, {"tp": t}

    other_core = {"ctx": y_hi * 2 + 1 - core}
    far = {"ctx": (1 - y_hi) * 2 + core}
    diagonal = {"ctx": (1 - y_hi) * 2 + 1 - core}
    other_ctx = y_hi * 2 + 1 - core
    far_ctx = (1 - y_hi) * 2 + core
    diagonal_ctx = (1 - y_hi) * 2 + 1 - core

    def remote(src, dst, ssem, rsem, device):
        return pltpu.make_async_remote_copy(
            src_ref=src, dst_ref=dst, send_sem=ssem, recv_sem=rsem, device_id=device, device_id_type=MESH
        )

    barrier = pltpu.get_barrier_semaphore()

    def greet(device):
        pl.semaphore_signal(barrier, inc=1, device_id=device, device_id_type=MESH)

    for e in Z_ORDER:
        greet(along_z(e)[1])
    for e in PLANE_ORDER:
        greet(plane(e)[1])
    greet(diagonal)
    greet(other_core)

    locals_ = [
        (hid_hbm.at[0], state.at[0]),
        (pk_hbm.at[pl.ds(0, 16)], k0.at[ctx]),
        (sk_hbm, span.at[core, x, y, 0]),
        (sv_hbm, span.at[core, x, y, 1]),
        (pk_hbm, kv.at[ctx, 0]),
        (pv_hbm, kv.at[ctx, 1]),
        (q_hbm, q),
        (wq_hbm, wq),
        (ck_hbm, kd.at[:, pl.ds(SPAN, CACHE)]),
        (cv_hbm, vd.at[:, pl.ds(SPAN, CACHE)]),
        (wo_hbm, wo),
    ]
    locals_ = [pltpu.make_async_copy(a, b, local_sem.at[i]) for i, (a, b) in enumerate(locals_)]
    for c in locals_:
        c.start()

    def hidden_copy(s, e):
        return remote(state.at[s], xall.at[s, tp], z_ssem.at[s, e], z_rsem.at[s, e], along_z(e)[1])

    def hidden_start(s):
        for e in Z_ORDER:
            hidden_copy(s, e).start()
        xall[s, tp] = state[s]

    def hidden_wait(s):
        for e in Z_ORDER:
            hidden_copy(s, e).wait()

    def pair_copy(s):
        return remote(part.at[s, 1 - core], pair.at[s], pr_ssem.at[s], pr_rsem.at[s], other_core)

    def rs_copy(s, e):
        t, device = plane(e)
        return remote(rs_send.at[s, t], rs_recv.at[s, me], rs_ssem.at[s, e[0], e[1]], rs_rsem.at[s, e[0], e[1]], device)

    def att_copy(s, e):
        return remote(att_send.at[s], att_all.at[s, core, me], at_ssem.at[s, e[0], e[1]], at_rsem.at[s, e[0], e[1]], plane(e)[1])

    def att_forward(s):
        return remote(att_all.at[s, core], att_all.at[s, core], fw_ssem.at[s], fw_rsem.at[s], other_core)

    def out_copy(s, e):
        t, device = along_z(e)
        block = ((t // 2) % 2 * 2 + t // 4) * 2 + t % 2
        return remote(z_send.at[s, block], z_recv.at[s, tp], rz_ssem.at[s, e], rz_rsem.at[s, e], device)

    k0_copies = [
        remote(k0.at[ctx], k0.at[ctx], k0_ssem.at[i], k0_rsem.at[i], device)
        for i, device in enumerate((other_core, far, diagonal))
    ]
    def span_first(e):
        piece = span.at[core, x, y]
        return (
            remote(piece, piece, s1_ssem.at[0, e], s1_rsem.at[0, e], along_x(e)),
            remote(piece, piece, s1_ssem.at[1, e], s1_rsem.at[1, e], along_y(e)),
        )

    def keys_on(d, e):
        piece = span.at[core, (x + d) % 4, y, 0]
        return remote(piece, piece, s2_ssem.at[0, d, e], s2_rsem.at[0, d, e], along_y(e))

    def values_on(d, e):
        piece = span.at[core, x, (y + d) % 4, 1]
        return remote(piece, piece, s2_ssem.at[1, d, e], s2_rsem.at[1, d, e], along_x(e))

    def span_core(d, e):
        piece = span.at[core, (x + d) % 4, (y + e) % 4]
        return remote(piece, piece, sf_ssem.at[d, e], sf_rsem.at[d, e], other_core)

    def span_open():
        for e in (1, 3, 2):
            for c in span_first(e):
                c.start()
        span_core(0, 0).start()

    def span_relay(*which):
        for d in which:
            along, across = span_first(d)
            along.wait()
            across.wait()
            for e in (1, 3, 2):
                keys_on(4 - d, e).start()
                values_on(4 - d, e).start()
            span_core(4 - d, 0).start()
            span_core(0, 4 - d).start()

    def span_close():
        for a in (3, 1, 2):
            for b in (3, 1, 2):
                keys_on(a, 4 - b).wait()
                values_on(b, 4 - a).wait()
                span_core(a, b).start()

    def span_done():
        for d in range(4):
            for e in range(4):
                span_core(d, e).wait()

    prefix_core = remote(kv.at[ctx], kv.at[ctx], pc_ssem, pc_rsem, other_core)

    def prefix_far(i):
        chunk = kv.at[ctx, :, pl.ds(i * CHUNK, CHUNK)]
        return remote(chunk, chunk, pf_ssem.at[i], pf_rsem.at[i], far)

    def prefix_far_start(first, last):
        for i in range(first, last):
            prefix_far(i).start()

    def prefix_forward(j):
        half = kv.at[far_ctx, :, pl.ds(j * UNIT, UNIT)]
        return remote(half, half, pd_ssem.at[j], pd_rsem.at[j], other_core)

    def prefix_relay(j):
        per = UNIT // CHUNK
        for i in range(j * per, (j + 1) * per):
            prefix_far(i).wait()
        prefix_forward(j).start()

    def project_rows(s, c):
        rows = jnp.concatenate([xall[s, pl.ds(c * 2, 2)], xall[s, pl.ds(4 + c * 2, 2)]], 0).reshape(128, 256)
        out = jnp.dot(rows, wq[...], preferred_element_type=F32).reshape(16, 8, 1280)
        part[s, c] = jnp.concatenate([out[:, :, :640], out[:, :, 640:]], 1).astype(BF16)

    def project(s):
        project_rows(s, 1 - core)
        pair_copy(s).start()
        project_rows(s, core)

    def scatter(s):
        pair_copy(s).wait()
        rs_send[s] = (part[s, core].astype(F32) + pair[s].astype(F32)).astype(BF16)

        for e in PLANE_ORDER:
            rs_copy(s, e).start()
        rs_recv[s, me] = rs_send[s, me]

    def gather_rows(s):
        for e in PLANE_ORDER:
            rs_copy(s, e).wait()
        total = jnp.sum(rs_recv[s].astype(F32), 0).astype(BF16).astype(F32)
        for i in range(5):
            heads[i] = total[0:8, i * HD:(i + 1) * HD]
        for i in range(3):
            heads[5 + i] = total[8:16, i * HD:(i + 1) * HD]
        new_kv[s, 0] = total[8:16, 3 * HD:4 * HD]
        new_kv[s, 1] = total[8:16, 4 * HD:5 * HD]
        spot = lax.broadcasted_iota(jnp.int32, (16, HD), 0)
        for r in range(DRW):
            for which, buffer in ((0, kd), (1, vd)):
                fresh = jnp.zeros((16, HD), F32)
                for t in range(s + 1):
                    fresh = jnp.where(spot == t, new_kv[t, which, pl.ds(r, 1), :], fresh)
                buffer[r, pl.ds(TAIL, 16)] = fresh.astype(BF16)

    def query_rows():
        return jnp.stack([heads[:, r, :] for r in range(DRW)], 0).astype(BF16)

    def attend_cache():
        late[...] = lax.dot_general(
            query_rows(), kd[:, SPAN:KEYS], (((2,), (2,)), ((0,), (0,))), preferred_element_type=F32
        )

    def attend(s):
        early = lax.dot_general(
            query_rows(), kd[:, 0:SPAN], (((2,), (2,)), ((0,), (0,))), preferred_element_type=F32
        )
        scores = jnp.concatenate([early, late[...]], 2) * SCALE + bias[...]
        if s == 0:
            spot = lax.broadcasted_iota(jnp.int32, (DRW, GROUP, KEYS), 2)
            scores = jnp.where(spot == TAIL + 1, NEGATIVE, scores)
        peak = jnp.max(scores, -1, keepdims=True)
        expon = jnp.exp(scores - peak)
        total = jnp.sum(expon, -1, keepdims=True)
        summed = lax.dot_general(
            expon.astype(BF16), vd[...], (((2,), (1,)), ((0,), (0,))), preferred_element_type=F32
        )
        att_o[...] = summed / total
        for i in range(4):
            both = jnp.concatenate([att_o[:, i, :], att_o[:, 4 + i, :]], 0)
            att_send[s, :, i * HD:(i + 1) * HD] = both.astype(BF16)

        for e in PLANE_ORDER:
            att_copy(s, e).start()
        att_all[s, core, me] = att_send[s]

    def relay_attended(s):
        for e in PLANE_ORDER:
            att_copy(s, e).wait()
        att_forward(s).start()

    def out_project_rows(s, c):
        rows = att_all[s, c].astype(F32)
        left = rows[:, 0:8].reshape(128, 512).astype(BF16)
        right = rows[:, 8:16].reshape(128, 512).astype(BF16)
        out = jnp.dot(left, wo[0:512], preferred_element_type=F32)
        out = out + jnp.dot(right, wo[512:1024], preferred_element_type=F32)
        z_send[s, pl.ds(c * 4, 4)] = out.astype(BF16).reshape(4, 32, 256)

    def out_project(s):
        out_project_rows(s, core)
        att_forward(s).wait()
        out_project_rows(s, 1 - core)
        for e in Z_ORDER:
            out_copy(s, e).start()
        z_recv[s, tp] = z_send[s, ((tp // 2) % 2 * 2 + tp // 4) * 2 + tp % 2]

    def finish_step(s):
        for e in Z_ORDER:
            out_copy(s, e).wait()
        result = jnp.sum(z_recv[s].astype(F32), 0).astype(BF16)
        step_out[s] = result
        if s + 1 < STEPS:
            state[s + 1] = (state[s].astype(F32) + result.astype(F32)).astype(BF16)

    def pick_span():
        def body(r, _):
            c = row_context[me_rows + r]
            for k in range(2):
                for h in range(2):
                    at = (h * 2 + k) * 256
                    kd[r, pl.ds(at, 256)] = span[k, c // 2, h * 2 + c % 2, 0]
                    vd[r, pl.ds(at, 256)] = span[k, c // 2, h * 2 + c % 2, 1]
            return 0
        lax.fori_loop(0, DRW, body, 0)

    me_rows = (ctx * 8 + row) * DRW

    def decode_bias():
        spot = lax.broadcasted_iota(jnp.int32, (GROUP, KEYS), 1)

        def body(r, _):
            c = row_context[me_rows + r]
            valid = context_len[c] - prefix_len[c]
            live = cache_len[me_rows + r]
            end = jnp.where(spot < SPAN, valid, jnp.where(spot < TAIL, SPAN + live, TAIL + STEPS))
            bias[r] = jnp.where(spot < end, 0.0, NEGATIVE)
            kd[r, pl.ds(TAIL, 128)] = jnp.zeros((128, HD), BF16)
            vd[r, pl.ds(TAIL, 128)] = jnp.zeros((128, HD), BF16)
            return 0
        lax.fori_loop(0, DRW, body, 0)

    def prefill_start():
        m_ref[...] = jnp.full(m_ref.shape, NEGATIVE, F32)
        acc_ref[...] = jnp.zeros(acc_ref.shape, F32)
        at = lax.broadcasted_iota(jnp.int32, (256, SPAN), 0) + ctx * 256
        spot = lax.broadcasted_iota(jnp.int32, (256, SPAN), 1)
        valid = context_len[row] - prefix_len[row]
        span_bias[...] = jnp.where((spot <= at) & (spot < valid), 0.0, NEGATIVE)

    def prepare(piece, j, first):
        spot = lax.broadcasted_iota(jnp.int32, (UNIT, HD), 0) + (piece * PIECE + j * UNIT)
        live = spot < prefix_len[row]
        rows = pl.ds(j * UNIT, UNIT)
        kx[...] = jnp.where(live, kv[piece, 0, rows].astype(F32), first.astype(F32)).astype(BF16)
        vx[:, 0:HD] = jnp.where(live, kv[piece, 1, rows].astype(F32), 0.0).astype(BF16)
        vx[:, HD:2 * HD] = jnp.where(live, 1.0, 0.0).astype(BF16)

    def update(h, keys, values, mask):
        scores = nt_dot(q[:, h * HD:(h + 1) * HD], keys)
        if mask is not None:
            scores = scores + mask
        old = m_ref[h]
        new = jnp.maximum(old, jnp.max(scores, 1, keepdims=True))
        expon = jnp.exp2((scores - new[:, 0:1]) * (SCALE * LOG2E)).astype(BF16)
        rescale = jnp.exp2((old - new) * (SCALE * LOG2E))
        m_ref[h] = new
        acc_ref[h] = acc_ref[h] * jnp.concatenate([rescale, rescale], 1) + jnp.dot(
            expon, values, preferred_element_type=F32
        )

    def forget_dead():
        m_ref[...] = jnp.where(ctx * PIECE < prefix_len[row], m_ref[...], NEGATIVE)

    def first_unit(j):
        prepare(ctx, j, kv[ctx, 0, 0:1, :])
        for h in range(GROUP):
            update(h, kx[...], vx[...], None)

    def unit(piece, j):
        prepare(piece, j, k0[0, 0:1, :])
        for h in range(GROUP):
            update(h, kx[...], vx[...], None)

    def span_unit():
        for i in range(4):
            kx[pl.ds(i * 256, 256)] = span[i % 2, x, i // 2 * 2 + y_lo, 0]
            vx[pl.ds(i * 256, 256), 0:HD] = span[i % 2, x, i // 2 * 2 + y_lo, 1]
        vx[:, HD:2 * HD] = jnp.ones((SPAN, HD), BF16)

        for h in range(GROUP):
            update(h, kx[...], vx[...], span_bias[...])

    def prefill_end():
        for h in range(GROUP):
            acc = acc_ref[h]
            pre_out[:, h * HD:(h + 1) * HD] = (acc[:, 0:HD] / acc[:, HD:2 * HD]).astype(BF16)

    for i in range(4):
        locals_[i].wait()
    pl.semaphore_wait(barrier, 24)
    hidden_start(0)
    for c in k0_copies:
        c.start()
    span_open()
    for i in range(4, 7):
        locals_[i].wait()
    prefix_core.start()
    prefill_start()
    first_unit(0)
    locals_[7].wait()
    hidden_wait(0)
    project(0)
    span_relay(1, 3)
    scatter(0)
    span_relay(2)
    first_unit(1)
    forget_dead()
    for c in k0_copies:
        c.wait()
    prefix_core.wait()
    unit(other_ctx, 0)
    decode_bias()
    for i in range(8, 11):
        locals_[i].wait()
    span_close()
    gather_rows(0)
    prefix_far_start(0, 2)
    attend_cache()
    span_done()
    pick_span()
    attend(0)
    unit(other_ctx, 1)
    relay_attended(0)
    prefix_far_start(2, 7)
    out_project(0)
    finish_step(0)
    hidden_start(1)
    prefix_relay(0)
    unit(far_ctx, 0)
    hidden_wait(1)
    project(1)
    prefix_forward(0).wait()
    scatter(1)
    unit(diagonal_ctx, 0)
    gather_rows(1)
    prefix_far_start(7, 8)
    attend_cache()
    attend(1)
    span_unit()
    relay_attended(1)
    prefix_relay(1)
    out_project(1)
    unit(far_ctx, 1)
    prefix_forward(1).wait()
    unit(diagonal_ctx, 1)
    prefill_end()
    finish_step(1)


def hand_on(pre, steps, pre_out, steps_out):
    pre_out[0] = pre[...]
    steps_out[...] = steps[...]


def local(
    prefill_query, prefix_keys, prefix_values, span_keys, span_values, prefix_len, context_len,
    hidden, qkv_weight, out_weight, cache_keys, cache_values, row_context, cache_len,
):
    dma = pltpu.SemaphoreType.DMA
    smem = pl.BlockSpec(memory_space=pltpu.SMEM)
    anywhere = pl.BlockSpec(memory_space=pl.ANY)
    vmem = pl.BlockSpec(memory_space=pltpu.VMEM)
    pre, steps = pl.pallas_call(
        kernel,
        out_shape=(
            jax.ShapeDtypeStruct((256, GROUP * HD), BF16),
            jax.ShapeDtypeStruct((STEPS, 32, 256), BF16),
        ),
        in_specs=[smem] * 4 + [anywhere] * 10,
        out_specs=(vmem, vmem),
        scratch_shapes=[
            pltpu.VMEM((256, GROUP * HD), BF16),
            pltpu.VMEM((4, 2, PIECE, HD), BF16),
            pltpu.VMEM((UNIT, HD), BF16),
            pltpu.VMEM((UNIT, 2 * HD), BF16),
            pltpu.VMEM((4, 16, HD), BF16),
            pltpu.VMEM((2, 4, 4, 2, 256, HD), BF16),
            pltpu.VMEM((DRW, KEYS, HD), BF16),
            pltpu.VMEM((DRW, KEYS, HD), BF16),
            pltpu.VMEM((DRW, GROUP, KEYS), F32),
            pltpu.VMEM((256, SPAN), F32),
            pltpu.VMEM((256, 1280), BF16),
            pltpu.VMEM((1024, 256), BF16),
            pltpu.VMEM((STEPS, 32, 256), BF16),
            pltpu.VMEM((STEPS, 8, 32, 256), BF16),
            pltpu.VMEM((STEPS, 2, 16, 16, 640), BF16),
            pltpu.VMEM((STEPS, 16, 16, 640), BF16),
            pltpu.VMEM((STEPS, 16, 16, 640), BF16),
            pltpu.VMEM((STEPS, 16, 16, 640), BF16),
            pltpu.VMEM((GROUP, DRW, HD), F32),
            pltpu.VMEM((STEPS, 2, DRW, HD), F32),
            pltpu.VMEM((DRW, GROUP, HD), F32),
            pltpu.VMEM((STEPS, 16, 512), BF16),
            pltpu.VMEM((STEPS, 2, 16, 16, 512), BF16),
            pltpu.VMEM((STEPS, 8, 32, 256), BF16),
            pltpu.VMEM((STEPS, 8, 32, 256), BF16),
            pltpu.VMEM((DRW, GROUP, KEYS - SPAN), F32),
            pltpu.VMEM((GROUP, 256, HD), F32),
            pltpu.VMEM((GROUP, 256, 2 * HD), F32),
            dma((11,)),
            dma((STEPS, 8)), dma((STEPS, 8)),
            dma((STEPS,)), dma((STEPS,)),
            dma((STEPS, 4, 4)), dma((STEPS, 4, 4)),
            dma((STEPS, 4, 4)), dma((STEPS, 4, 4)),
            dma((STEPS,)), dma((STEPS,)),
            dma((STEPS, 8)), dma((STEPS, 8)),
            dma((3,)), dma((3,)),
            dma((2, 4)), dma((2, 4)),
            dma((2, 4, 4)), dma((2, 4, 4)),
            dma((4, 4)), dma((4, 4)),
            dma, dma,
            dma((PIECE // CHUNK,)), dma((PIECE // CHUNK,)),
            dma((2,)), dma((2,)),
        ],
        compiler_params=pltpu.CompilerParams(
            collective_id=0, has_side_effects=True, vmem_limit_bytes=56 * 1024 * 1024
        ),
        name="layer",
    )(
        prefix_len, context_len, row_context, cache_len,
        prefill_query[0], prefix_keys[0], prefix_values[0], span_keys[0], span_values[0],
        hidden[None], qkv_weight.reshape(256, 1280), out_weight, cache_keys, cache_values,
    )
    return pl.pallas_call(
        hand_on,
        out_shape=(
            jax.ShapeDtypeStruct((1, 256, GROUP * HD), BF16),
            jax.ShapeDtypeStruct((STEPS, 32, 256), BF16),
        ),
        in_specs=[vmem, vmem],
        out_specs=(vmem, vmem),
        name="hand_on",
    )(pre, steps)


def solution(mesh):
    in_specs = (
        P("row", "ctx", "tp"),
        P("row", "ctx", "tp"),
        P("row", "ctx", "tp"),
        P("row", "ctx", "tp"),
        P("row", "ctx", "tp"),
        P(),
        P(),
        P("tp", ("ctx", "row")),
        P(("ctx", "row"), "tp", None),
        P("tp", ("ctx", "row")),
        P(("ctx", "row"), None, "tp"),
        P(("ctx", "row"), None, "tp"),
        P(),
        P(),
    )
    out_specs = (P("row", "ctx", "tp"), P(None, "tp", ("ctx", "row")))
    return jax.shard_map(local, mesh=mesh, in_specs=in_specs, out_specs=out_specs, check_vma=False)
```

```python
import jax
import jax.numpy as jnp
from jax import lax
from jax.experimental import pallas as pl
from jax.experimental.pallas import tpu as pltpu
from jax.sharding import PartitionSpec as P

HD = 128
GROUP = 8
STEPS = 2
SPAN = 1024
CACHE = 1024
PIECE = 2048
DRW = 8
TAIL = 2 * SPAN
KEYS = TAIL + 128
UNIT = 1024
CHUNK = 256
NEGATIVE = -1e30
SCALE = HD ** (-0.5)
LOG2E = 1.4426950408889634
F32 = jnp.float32
BF16 = jnp.bfloat16
MESH = pl.DeviceIdType.MESH
Z_ORDER = (4, 3, 5, 2, 6, 1, 7)
PLANE_ORDER = (
    (2, 2), (2, 1), (2, 3), (1, 2), (3, 2), (2, 0), (0, 2), (1, 1), (1, 3), (3, 1), (3, 3), (1, 0), (3, 0), (0, 1), (0, 3)
)


def nt_dot(a, b):
    return lax.dot_general(a, b, (((1,), (1,)), ((), ())), preferred_element_type=F32)


def kernel(
    prefix_len_any, context_len_any, row_context_any, cache_len_any,
    q_hbm, pk_hbm, pv_hbm, sk_hbm, sv_hbm, hid_hbm, wq_hbm, wo_hbm, ck_hbm, cv_hbm,
    pre_any, step_any,
    prefix_len, context_len, row_context, cache_len, pre_out, step_out, q, kv, kx, vx, k0, span, kd, vd, bias, span_bias, wq, wo,
    state, xall, part, pair, rs_send, rs_recv, heads, new_kv, att_o, att_send, att_all, z_send, z_recv, late,
    m_ref, acc_ref,
    local_sem, z_ssem, z_rsem, pr_ssem, pr_rsem, rs_ssem, rs_rsem, at_ssem, at_rsem, fw_ssem, fw_rsem,
    rz_ssem, rz_rsem, k0_ssem, k0_rsem, s1_ssem, s1_rsem, s2_ssem, s2_rsem, sf_ssem, sf_rsem,
    pc_ssem, pc_rsem, pf_ssem, pf_rsem, pd_ssem, pd_rsem,
):
    ctx = lax.axis_index("ctx")
    row = lax.axis_index("row")
    tp = lax.axis_index("tp")
    core = ctx % 2
    y_hi = ctx // 2
    x = row // 2
    y_lo = row % 2
    y = y_hi * 2 + y_lo
    me = y_hi * 8 + row

    def plane(e):
        to_x, to_y = (x + e[0]) % 4, (y + e[1]) % 4
        return (to_y // 2) * 8 + to_x * 2 + to_y % 2, {"ctx": (to_y // 2) * 2 + core, "row": to_x * 2 + to_y % 2}

    def along_y(e):
        t = (y + e) % 4
        return {"ctx": (t // 2) * 2 + core, "row": x * 2 + t % 2}

    def along_x(e):
        return {"row": ((x + e) % 4) * 2 + y_lo}

    def along_z(e):
        t = (tp + e) % 8
        return t, {"tp": t}

    other_core = {"ctx": y_hi * 2 + 1 - core}
    far = {"ctx": (1 - y_hi) * 2 + core}
    diagonal = {"ctx": (1 - y_hi) * 2 + 1 - core}
    other_ctx = y_hi * 2 + 1 - core
    far_ctx = (1 - y_hi) * 2 + core
    diagonal_ctx = (1 - y_hi) * 2 + 1 - core

    def wait_bytes(ref, sem):
        pltpu.make_async_copy(ref, ref, sem).wait()

    def remote(src, dst, ssem, rsem, device):
        return pltpu.make_async_remote_copy(
            src_ref=src, dst_ref=dst, send_sem=ssem, recv_sem=rsem, device_id=device, device_id_type=MESH
        )

    barrier = pltpu.get_barrier_semaphore()

    def greet(device):
        pl.semaphore_signal(barrier, inc=1, device_id=device, device_id_type=MESH)

    for e in Z_ORDER:
        greet(along_z(e)[1])
    for e in PLANE_ORDER:
        greet(plane(e)[1])
    greet(diagonal)
    greet(other_core)

    locals_ = [
        (hid_hbm.at[0], state.at[0]),
        (pk_hbm.at[pl.ds(0, 16)], k0.at[ctx]),
        (sk_hbm, span.at[core, x, y, 0]),
        (sv_hbm, span.at[core, x, y, 1]),
        (pk_hbm, kv.at[ctx, 0]),
        (pv_hbm, kv.at[ctx, 1]),
        (q_hbm, q),
        (wq_hbm, wq),
        (ck_hbm, kd.at[:, pl.ds(SPAN, CACHE)]),
        (cv_hbm, vd.at[:, pl.ds(SPAN, CACHE)]),
        (wo_hbm, wo),
        (prefix_len_any, prefix_len),
        (context_len_any, context_len),
        (row_context_any, row_context),
        (cache_len_any, cache_len),
    ]
    locals_ = [pltpu.make_async_copy(a, b, local_sem.at[i]) for i, (a, b) in enumerate(locals_)]
    for c in locals_:
        c.start()
    results = [
        pltpu.make_async_copy(step_out.at[0], step_any.at[0], local_sem.at[15]),
        pltpu.make_async_copy(step_out.at[1], step_any.at[1], local_sem.at[16]),
        pltpu.make_async_copy(pre_out, pre_any, local_sem.at[17]),
    ]

    def hidden_copy(s, e):
        return remote(state.at[s], xall.at[s, tp], z_ssem.at[s], z_rsem.at[s], along_z(e)[1])

    def hidden_start(s):
        for e in Z_ORDER:
            hidden_copy(s, e).start()
        xall[s, tp] = state[s]

    def hidden_wait(s):
        wait_bytes(xall.at[s, pl.ds(0, 7)], z_ssem.at[s])
        wait_bytes(xall.at[s, pl.ds(0, 7)], z_rsem.at[s])

    def pair_copy(s):
        return remote(part.at[s, 1 - core], pair.at[s], pr_ssem.at[s], pr_rsem.at[s], other_core)

    def rs_copy(s, e):
        t, device = plane(e)
        return remote(rs_send.at[s, t], rs_recv.at[s, me], rs_ssem.at[s], rs_rsem.at[s], device)

    def att_copy(s, e):
        return remote(att_send.at[s], att_all.at[s, core, me], at_ssem.at[s], at_rsem.at[s], plane(e)[1])

    def att_forward(s):
        return remote(att_all.at[s, core], att_all.at[s, core], fw_ssem.at[s], fw_rsem.at[s], other_core)

    def out_copy(s, e):
        t, device = along_z(e)
        block = ((t // 2) % 2 * 2 + t // 4) * 2 + t % 2
        return remote(z_send.at[s, block], z_recv.at[s, tp], rz_ssem.at[s], rz_rsem.at[s], device)

    k0_copies = [
        remote(k0.at[ctx], k0.at[ctx], k0_ssem, k0_rsem, device)
        for device in (other_core, far, diagonal)
    ]
    def span_first(e):
        piece = span.at[core, x, y]
        return (
            remote(piece, piece, s1_ssem.at[0, e - 1], s1_rsem.at[0, e - 1], along_x(e)),
            remote(piece, piece, s1_ssem.at[1, e - 1], s1_rsem.at[1, e - 1], along_y(e)),
        )

    def keys_on(d, e):
        piece = span.at[core, (x + d) % 4, y, 0]
        return remote(piece, piece, s2_ssem.at[0, d - 1, e - 1], s2_rsem.at[0, d - 1, e - 1], along_y(e))

    def values_on(d, e):
        piece = span.at[core, x, (y + d) % 4, 1]
        return remote(piece, piece, s2_ssem.at[1, d - 1, e - 1], s2_rsem.at[1, d - 1, e - 1], along_x(e))

    def span_core(d, e):
        piece = span.at[core, (x + d) % 4, (y + e) % 4]
        return remote(piece, piece, sf_ssem, sf_rsem, other_core)

    def span_open():
        for e in (1, 3, 2):
            for c in span_first(e):
                c.start()
        span_core(0, 0).start()

    def span_relay(*which):
        for d in which:
            along, across = span_first(d)
            along.wait()
            across.wait()
            for e in (1, 3, 2):
                keys_on(4 - d, e).start()
                values_on(4 - d, e).start()
            span_core(4 - d, 0).start()
            span_core(0, 4 - d).start()

    def span_close():
        for a in (3, 1, 2):
            for b in (3, 1, 2):
                keys_on(a, 4 - b).wait()
                values_on(b, 4 - a).wait()
                span_core(a, b).start()

    def span_done():
        wait_bytes(span.at[core], sf_ssem)
        wait_bytes(span.at[1 - core], sf_rsem)

    prefix_core = remote(kv.at[ctx], kv.at[ctx], pc_ssem, pc_rsem, other_core)

    def prefix_far(i):
        chunk = kv.at[ctx, :, pl.ds(i * CHUNK, CHUNK)]
        return remote(chunk, chunk, pf_ssem.at[i], pf_rsem.at[i], far)

    def prefix_far_start(first, last):
        for i in range(first, last):
            prefix_far(i).start()

    onward = ((0, 4), (4, 7), (7, 8))

    def prefix_forward(j):
        first, last = onward[j]
        rows = kv.at[far_ctx, :, pl.ds(first * CHUNK, (last - first) * CHUNK)]
        return remote(rows, rows, pd_ssem.at[j], pd_rsem.at[j], other_core)

    def prefix_relay(j):
        for i in range(*onward[j]):
            prefix_far(i).wait()
        prefix_forward(j).start()

    def project_rows(s, c):
        rows = jnp.concatenate([xall[s, pl.ds(c * 2, 2)], xall[s, pl.ds(4 + c * 2, 2)]], 0).reshape(128, 256)
        out = jnp.dot(rows, wq[...], preferred_element_type=F32).reshape(16, 8, 1280)
        part[s, c] = jnp.concatenate([out[:, :, :640], out[:, :, 640:]], 1).astype(BF16)

    def project(s):
        project_rows(s, 1 - core)
        pair_copy(s).start()
        project_rows(s, core)

    def scatter(s):
        pair_copy(s).wait()
        rs_send[s] = (part[s, core].astype(F32) + pair[s].astype(F32)).astype(BF16)

        for e in PLANE_ORDER:
            rs_copy(s, e).start()
        rs_recv[s, me] = rs_send[s, me]

    def gather_rows(s):
        wait_bytes(rs_recv.at[s, pl.ds(0, 15)], rs_ssem.at[s])
        wait_bytes(rs_recv.at[s, pl.ds(0, 15)], rs_rsem.at[s])
        total = jnp.sum(rs_recv[s].astype(F32), 0).astype(BF16).astype(F32)
        for i in range(5):
            heads[i] = total[0:8, i * HD:(i + 1) * HD]
        for i in range(3):
            heads[5 + i] = total[8:16, i * HD:(i + 1) * HD]
        new_kv[s, 0] = total[8:16, 3 * HD:4 * HD]
        new_kv[s, 1] = total[8:16, 4 * HD:5 * HD]
        spot = lax.broadcasted_iota(jnp.int32, (16, HD), 0)
        for r in range(DRW):
            for which, buffer in ((0, kd), (1, vd)):
                fresh = jnp.zeros((16, HD), F32)
                for t in range(s + 1):
                    fresh = jnp.where(spot == t, new_kv[t, which, pl.ds(r, 1), :], fresh)
                buffer[r, pl.ds(TAIL, 16)] = fresh.astype(BF16)

    def query_rows():
        return jnp.stack([heads[:, r, :] for r in range(DRW)], 0).astype(BF16)

    def attend_cache():
        late[...] = lax.dot_general(
            query_rows(), kd[:, SPAN:KEYS], (((2,), (2,)), ((0,), (0,))), preferred_element_type=F32
        )

    def attend(s):
        early = lax.dot_general(
            query_rows(), kd[:, 0:SPAN], (((2,), (2,)), ((0,), (0,))), preferred_element_type=F32
        )
        scores = jnp.concatenate([early, late[...]], 2) * SCALE + bias[...]
        if s == 0:
            spot = lax.broadcasted_iota(jnp.int32, (DRW, GROUP, KEYS), 2)
            scores = jnp.where(spot == TAIL + 1, NEGATIVE, scores)
        peak = jnp.max(scores, -1, keepdims=True)
        expon = jnp.exp(scores - peak)
        total = jnp.sum(expon, -1, keepdims=True)
        summed = lax.dot_general(
            expon.astype(BF16), vd[...], (((2,), (1,)), ((0,), (0,))), preferred_element_type=F32
        )
        att_o[...] = summed / total
        for i in range(4):
            both = jnp.concatenate([att_o[:, i, :], att_o[:, 4 + i, :]], 0)
            att_send[s, :, i * HD:(i + 1) * HD] = both.astype(BF16)

        for e in PLANE_ORDER:
            att_copy(s, e).start()
        att_all[s, core, me] = att_send[s]

    def relay_attended(s):
        wait_bytes(att_all.at[s, core, pl.ds(0, 15)], at_ssem.at[s])
        wait_bytes(att_all.at[s, core, pl.ds(0, 15)], at_rsem.at[s])
        att_forward(s).start()

    def out_project_rows(s, c):
        rows = att_all[s, c].astype(F32)
        left = rows[:, 0:8].reshape(128, 512).astype(BF16)
        right = rows[:, 8:16].reshape(128, 512).astype(BF16)
        out = jnp.dot(left, wo[0:512], preferred_element_type=F32)
        out = out + jnp.dot(right, wo[512:1024], preferred_element_type=F32)
        z_send[s, pl.ds(c * 4, 4)] = out.astype(BF16).reshape(4, 32, 256)

    def out_project(s):
        out_project_rows(s, core)
        att_forward(s).wait()
        out_project_rows(s, 1 - core)
        for e in Z_ORDER:
            out_copy(s, e).start()
        z_recv[s, tp] = z_send[s, ((tp // 2) % 2 * 2 + tp // 4) * 2 + tp % 2]

    def finish_step(s):
        wait_bytes(z_recv.at[s, pl.ds(0, 7)], rz_ssem.at[s])
        wait_bytes(z_recv.at[s, pl.ds(0, 7)], rz_rsem.at[s])
        result = jnp.sum(z_recv[s].astype(F32), 0).astype(BF16)
        step_out[s] = result
        if s + 1 < STEPS:
            state[s + 1] = (state[s].astype(F32) + result.astype(F32)).astype(BF16)

    def pick_span():
        def body(r, _):
            c = row_context[me_rows + r]
            for k in range(2):
                for h in range(2):
                    at = (h * 2 + k) * 256
                    kd[r, pl.ds(at, 256)] = span[k, c // 2, h * 2 + c % 2, 0]
                    vd[r, pl.ds(at, 256)] = span[k, c // 2, h * 2 + c % 2, 1]
            return 0
        lax.fori_loop(0, DRW, body, 0)

    me_rows = (ctx * 8 + row) * DRW

    def decode_bias():
        spot = lax.broadcasted_iota(jnp.int32, (GROUP, KEYS), 1)

        def body(r, _):
            c = row_context[me_rows + r]
            valid = context_len[c] - prefix_len[c]
            live = cache_len[me_rows + r]
            end = jnp.where(spot < SPAN, valid, jnp.where(spot < TAIL, SPAN + live, TAIL + STEPS))
            bias[r] = jnp.where(spot < end, 0.0, NEGATIVE)
            kd[r, pl.ds(TAIL, 128)] = jnp.zeros((128, HD), BF16)
            vd[r, pl.ds(TAIL, 128)] = jnp.zeros((128, HD), BF16)
            return 0
        lax.fori_loop(0, DRW, body, 0)

    def prefill_start():
        m_ref[...] = jnp.full(m_ref.shape, NEGATIVE, F32)
        acc_ref[...] = jnp.zeros(acc_ref.shape, F32)
        at = lax.broadcasted_iota(jnp.int32, (256, SPAN), 0) + ctx * 256
        spot = lax.broadcasted_iota(jnp.int32, (256, SPAN), 1)
        valid = context_len[row] - prefix_len[row]
        span_bias[...] = jnp.where((spot <= at) & (spot < valid), 0.0, NEGATIVE)

    def prepare(blocks, first):
        at = 0
        for piece, start, n in blocks:
            live = lax.broadcasted_iota(jnp.int32, (n, HD), 0) + (piece * PIECE + start) < prefix_len[row]
            rows, to = pl.ds(start, n), pl.ds(at, n)
            kx[to] = jnp.where(live, kv[piece, 0, rows].astype(F32), first.astype(F32)).astype(BF16)
            vx[to, 0:HD] = jnp.where(live, kv[piece, 1, rows].astype(F32), 0.0).astype(BF16)
            vx[to, HD:2 * HD] = jnp.where(live, 1.0, 0.0).astype(BF16)
            at += n

    def update(h, keys, values, mask):
        scores = nt_dot(q[:, h * HD:(h + 1) * HD], keys)
        if mask is not None:
            scores = scores + mask
        old = m_ref[h]
        new = jnp.maximum(old, jnp.max(scores, 1, keepdims=True))
        expon = jnp.exp2((scores - new[:, 0:1]) * (SCALE * LOG2E)).astype(BF16)
        rescale = jnp.exp2((old - new) * (SCALE * LOG2E))
        m_ref[h] = new
        acc_ref[h] = acc_ref[h] * jnp.concatenate([rescale, rescale], 1) + jnp.dot(
            expon, values, preferred_element_type=F32
        )

    def forget_dead():
        m_ref[...] = jnp.where(ctx * PIECE < prefix_len[row], m_ref[...], NEGATIVE)

    def first_unit(j):
        prepare([(ctx, j * UNIT, UNIT)], kv[ctx, 0, 0:1, :])
        for h in range(GROUP):
            update(h, kx[...], vx[...], None)

    def unit(*blocks):
        prepare(blocks, k0[0, 0:1, :])
        for h in range(GROUP):
            update(h, kx[...], vx[...], None)

    def span_unit():
        for i in range(4):
            kx[pl.ds(i * 256, 256)] = span[i % 2, x, i // 2 * 2 + y_lo, 0]
            vx[pl.ds(i * 256, 256), 0:HD] = span[i % 2, x, i // 2 * 2 + y_lo, 1]
        vx[:, HD:2 * HD] = jnp.ones((SPAN, HD), BF16)

        for h in range(GROUP):
            update(h, kx[...], vx[...], span_bias[...])

    def prefill_end():
        for h in range(GROUP):
            acc = acc_ref[h]
            pre_out[:, h * HD:(h + 1) * HD] = (acc[:, 0:HD] / acc[:, HD:2 * HD]).astype(BF16)

    for i in range(4):
        locals_[i].wait()
    pl.semaphore_wait(barrier, 24)
    hidden_start(0)
    for c in k0_copies:
        c.start()
    span_open()
    for i in (4, 5, 6, 11, 12, 13, 14):
        locals_[i].wait()
    prefix_core.start()
    prefill_start()
    first_unit(0)
    locals_[7].wait()
    hidden_wait(0)
    project(0)
    span_relay(1, 3)
    scatter(0)
    span_relay(2)
    first_unit(1)
    forget_dead()
    wait_bytes(k0.at[pl.ds(0, 3)], k0_ssem)
    wait_bytes(k0.at[pl.ds(0, 3)], k0_rsem)
    prefix_core.wait()
    unit((other_ctx, 0, UNIT))
    decode_bias()
    for i in range(8, 11):
        locals_[i].wait()
    span_close()
    gather_rows(0)
    prefix_far_start(0, 2)
    attend_cache()
    span_done()
    pick_span()
    attend(0)
    unit((other_ctx, UNIT, UNIT))
    relay_attended(0)
    prefix_far_start(2, 7)
    out_project(0)
    span_unit()
    finish_step(0)
    results[0].start()
    hidden_start(1)
    prefix_relay(0)
    unit((far_ctx, 0, UNIT))
    hidden_wait(1)
    project(1)
    prefix_forward(0).wait()
    scatter(1)
    unit((diagonal_ctx, 0, UNIT))
    prefix_relay(1)
    gather_rows(1)
    prefix_far_start(7, 8)
    attend_cache()
    attend(1)
    prefix_forward(1).wait()
    unit((far_ctx, 4 * CHUNK, 3 * CHUNK), (diagonal_ctx, 4 * CHUNK, CHUNK))
    relay_attended(1)
    prefix_relay(2)
    out_project(1)
    prefix_forward(2).wait()
    unit((far_ctx, 7 * CHUNK, CHUNK), (diagonal_ctx, 5 * CHUNK, 3 * CHUNK))
    prefill_end()
    results[2].start()
    finish_step(1)
    results[1].start()
    for c in results:
        c.wait()


def hand_on(pre, steps, pre_out, steps_out):
    pre_out[0] = pre[...]
    steps_out[...] = steps[...]


def local(
    prefill_query, prefix_keys, prefix_values, span_keys, span_values, prefix_len, context_len,
    hidden, qkv_weight, out_weight, cache_keys, cache_values, row_context, cache_len,
):
    dma = pltpu.SemaphoreType.DMA
    anywhere = pl.BlockSpec(memory_space=pl.ANY)
    vmem = pl.BlockSpec(memory_space=pltpu.VMEM)
    pre, steps = pl.pallas_call(
        kernel,
        out_shape=(
            jax.ShapeDtypeStruct((256, GROUP * HD), BF16),
            jax.ShapeDtypeStruct((STEPS, 32, 256), BF16),
        ),
        in_specs=[anywhere] * 14,
        out_specs=(anywhere, anywhere),
        scratch_shapes=[
            pltpu.SMEM((8,), jnp.int32),
            pltpu.SMEM((8,), jnp.int32),
            pltpu.SMEM((256,), jnp.int32),
            pltpu.SMEM((256,), jnp.int32),
            pltpu.VMEM((256, GROUP * HD), BF16),
            pltpu.VMEM((STEPS, 32, 256), BF16),
            pltpu.VMEM((256, GROUP * HD), BF16),
            pltpu.VMEM((4, 2, PIECE, HD), BF16),
            pltpu.VMEM((UNIT, HD), BF16),
            pltpu.VMEM((UNIT, 2 * HD), BF16),
            pltpu.VMEM((4, 16, HD), BF16),
            pltpu.VMEM((2, 4, 4, 2, 256, HD), BF16),
            pltpu.VMEM((DRW, KEYS, HD), BF16),
            pltpu.VMEM((DRW, KEYS, HD), BF16),
            pltpu.VMEM((DRW, GROUP, KEYS), F32),
            pltpu.VMEM((256, SPAN), F32),
            pltpu.VMEM((256, 1280), BF16),
            pltpu.VMEM((1024, 256), BF16),
            pltpu.VMEM((STEPS, 32, 256), BF16),
            pltpu.VMEM((STEPS, 8, 32, 256), BF16),
            pltpu.VMEM((STEPS, 2, 16, 16, 640), BF16),
            pltpu.VMEM((STEPS, 16, 16, 640), BF16),
            pltpu.VMEM((STEPS, 16, 16, 640), BF16),
            pltpu.VMEM((STEPS, 16, 16, 640), BF16),
            pltpu.VMEM((GROUP, DRW, HD), F32),
            pltpu.VMEM((STEPS, 2, DRW, HD), F32),
            pltpu.VMEM((DRW, GROUP, HD), F32),
            pltpu.VMEM((STEPS, 16, 512), BF16),
            pltpu.VMEM((STEPS, 2, 16, 16, 512), BF16),
            pltpu.VMEM((STEPS, 8, 32, 256), BF16),
            pltpu.VMEM((STEPS, 8, 32, 256), BF16),
            pltpu.VMEM((DRW, GROUP, KEYS - SPAN), F32),
            pltpu.VMEM((GROUP, 256, HD), F32),
            pltpu.VMEM((GROUP, 256, 2 * HD), F32),
            dma((18,)),
            dma((STEPS,)), dma((STEPS,)),
            dma((STEPS,)), dma((STEPS,)),
            dma((STEPS,)), dma((STEPS,)),
            dma((STEPS,)), dma((STEPS,)),
            dma((STEPS,)), dma((STEPS,)),
            dma((STEPS,)), dma((STEPS,)),
            dma, dma,
            dma((2, 3)), dma((2, 3)),
            dma((2, 3, 3)), dma((2, 3, 3)),
            dma, dma,
            dma, dma,
            dma((PIECE // CHUNK,)), dma((PIECE // CHUNK,)),
            dma((3,)), dma((3,)),
        ],
        compiler_params=pltpu.CompilerParams(
            collective_id=0, has_side_effects=True, vmem_limit_bytes=56 * 1024 * 1024
        ),
        name="layer",
    )(
        prefix_len, context_len, row_context, cache_len,
        prefill_query[0], prefix_keys[0], prefix_values[0], span_keys[0], span_values[0],
        hidden[None], qkv_weight.reshape(256, 1280), out_weight, cache_keys, cache_values,
    )
    return pl.pallas_call(
        hand_on,
        out_shape=(
            jax.ShapeDtypeStruct((1, 256, GROUP * HD), BF16),
            jax.ShapeDtypeStruct((STEPS, 32, 256), BF16),
        ),
        in_specs=[vmem, vmem],
        out_specs=(vmem, vmem),
        name="hand_on",
    )(pre, steps)


def solution(mesh):
    in_specs = (
        P("row", "ctx", "tp"),
        P("row", "ctx", "tp"),
        P("row", "ctx", "tp"),
        P("row", "ctx", "tp"),
        P("row", "ctx", "tp"),
        P(),
        P(),
        P("tp", ("ctx", "row")),
        P(("ctx", "row"), "tp", None),
        P("tp", ("ctx", "row")),
        P(("ctx", "row"), None, "tp"),
        P(("ctx", "row"), None, "tp"),
        P(),
        P(),
    )
    out_specs = (P("row", "ctx", "tp"), P(None, "tp", ("ctx", "row")))
    return jax.shard_map(local, mesh=mesh, in_specs=in_specs, out_specs=out_specs, check_vma=False)
```
